32 devices in a mesh: dp: 4 (over x, core), seq: 2 (over y), tensor: 4 (over z).
Axes of the slice: x: 2, y: 2, z: 4, core: 2. Of those that a mesh axis runs over, the one named last changes fastest.
Arguments:
- frames: bfloat16 [4, 1024, 768], P('dp', 'seq'), may hold values from -6 to 6
- cotangent: bfloat16 [4, 1024, 768], P('dp', 'seq'), may hold values from -6 to 6
- heads_weight: float32 [2, 768, 3, 768], P(None, ('dp', 'seq'), None, 'tensor'), may hold values from -0.3125 to 0.3125
- merge_weight: float32 [2, 768, 768], P(None, ('dp', 'seq'), 'tensor'), may hold values from -0.21875 to 0.21875
- expand_weight: float32 [2, 768, 4, 768], P(None, ('dp', 'seq'), None, 'tensor'), may hold values from -0.21875 to 0.21875
- shrink_weight: float32 [2, 768, 4, 768], P(None, ('dp', 'seq'), None, 'tensor'), may hold values from -0.21875 to 0.21875
- shared_vectors: float32 [2, 6, 768], replicated, may hold values from -1.2 to 1.2, as said below
- split_vectors: float32 [2, 6, 768], P(None, None, 'tensor'), may hold values from -1.2 to 1.2
- heads_first: float32 [2, 768, 3, 768], P(None, ('dp', 'seq'), None, 'tensor')
- heads_second: float32 [2, 768, 3, 768], P(None, ('dp', 'seq'), None, 'tensor'), as said below
- merge_first: float32 [2, 768, 768], P(None, ('dp', 'seq'), 'tensor')
- merge_second: float32 [2, 768, 768], P(None, ('dp', 'seq'), 'tensor'), as said below
- expand_first: float32 [2, 768, 4, 768], P(None, ('dp', 'seq'), None, 'tensor')
- expand_second: float32 [2, 768, 4, 768], P(None, ('dp', 'seq'), None, 'tensor'), as said below
- shrink_first: float32 [2, 768, 4, 768], P(None, ('dp', 'seq'), None, 'tensor')
- shrink_second: float32 [2, 768, 4, 768], P(None, ('dp', 'seq'), None, 'tensor'), as said below
- shared_first: float32 [2, 6, 768], replicated
- shared_second: float32 [2, 6, 768], replicated, as said below
- split_first: float32 [2, 6, 768], P(None, None, 'tensor')
- split_second: float32 [2, 6, 768], P(None, None, 'tensor'), as said below
Outputs:
- encoded: float32 [4, 1024, 768], P('dp', 'seq')
- input_grad: float32 [4, 1024, 768], P('dp', 'seq')
- heads_grad: float32 [2, 768, 3, 768], P(None, ('dp', 'seq'), None, 'tensor')
- heads_renewed: float32 [2, 768, 3, 768], P(None, ('dp', 'seq'), None, 'tensor')
- heads_updated: float32 [2, 768, 3, 768], P(None, ('dp', 'seq'), None, 'tensor')
- merge_grad: float32 [2, 768, 768], P(None, ('dp', 'seq'), 'tensor')
- merge_renewed: float32 [2, 768, 768], P(None, ('dp', 'seq'), 'tensor')
- merge_updated: float32 [2, 768, 768], P(None, ('dp', 'seq'), 'tensor')
- expand_grad: float32 [2, 768, 4, 768], P(None, ('dp', 'seq'), None, 'tensor')
- expand_renewed: float32 [2, 768, 4, 768], P(None, ('dp', 'seq'), None, 'tensor')
- expand_updated: float32 [2, 768, 4, 768], P(None, ('dp', 'seq'), None, 'tensor')
- shrink_grad: float32 [2, 768, 4, 768], P(None, ('dp', 'seq'), None, 'tensor')
- shrink_renewed: float32 [2, 768, 4, 768], P(None, ('dp', 'seq'), None, 'tensor')
- shrink_updated: float32 [2, 768, 4, 768], P(None, ('dp', 'seq'), None, 'tensor')
- shared_grad: float32 [2, 6, 768], replicated
- shared_renewed: float32 [2, 6, 768], replicated
- shared_updated: float32 [2, 6, 768], replicated
- split_grad: float32 [2, 6, 768], P(None, None, 'tensor')
- split_renewed: float32 [2, 6, 768], P(None, None, 'tensor')
- split_updated: float32 [2, 6, 768], P(None, None, 'tensor')
The draws below stay inside these ranges and needn't reach their ends.
Inputs may be any that keep to these rules, and one draw needn't show every extreme that they name: `shared_vectors`: norm gains lie in 0.8 to 1.2, the other rows are biases. `heads_second`: positive. `merge_second`: positive. `expand_second`: positive. `shrink_second`: positive. `shared_second`: positive. `split_second`: positive.
All inputs are finite; a program needn't handle non-finite values.
Results may differ from the reference program's by a relative error of at most 0.023.
Values may be sent and summed in bfloat16 or wider, within the bound.
A program may use at most 128 MiB of HBM per device.

```python
import math
import jax
import jax.numpy as jnp
from jax import lax

D = 768
HEADS = 12
HEAD_DIM = 64
FF = 3072
LAYERS = 2
STEP = 10
CLIPS = 4
FRAMES = 1024


def layer_factor(trailing):
    position = jnp.arange(LAYERS).reshape((LAYERS,) + (1,) * trailing)
    return jnp.where(position == LAYERS - 1, 1.0, 2.0).astype(jnp.float32)


def moment_draw(key, array_shape, factor):
    spread = 0.1 * math.sqrt(CLIPS * FRAMES) * factor * layer_factor(len(array_shape) - 1)
    return spread * jnp.clip(jax.random.normal(key, array_shape, jnp.float32), -4.0, 4.0)


def square_draw(key, array_shape, factor):
    level = factor * layer_factor(len(array_shape) - 1)
    level = 0.001 * CLIPS * FRAMES * level * level
    return level * jnp.exp(jax.random.uniform(key, array_shape, jnp.float32, 0.0, math.log(4.0)))


def shared_levels():
    return jnp.array([1.8, 1.6, 2.2, 1.9, 1.9, 1.2], jnp.float32).reshape(1, 6, 1)


def draw_heads_first(key, part):
    key = jax.random.fold_in(key, 11)
    return moment_draw(key, (LAYERS, D, 3, D), 0.6)


def draw_merge_first(key, part):
    key = jax.random.fold_in(key, 12)
    return moment_draw(key, (LAYERS, D, D), 0.95)


def draw_expand_first(key, part):
    key = jax.random.fold_in(key, 13)
    return moment_draw(key, (LAYERS, D, 4, D), 0.7)


def draw_shrink_first(key, part):
    key = jax.random.fold_in(key, 14)
    return moment_draw(key, (LAYERS, D, 4, D), 0.7)


def draw_shared_first(key, part):
    key = jax.random.fold_in(key, 15)
    return moment_draw(key, (LAYERS, 6, D), shared_levels())


def draw_split_first(key, part):
    key = jax.random.fold_in(key, 16)
    return moment_draw(key, (LAYERS, 6, D), 0.9)


def draw_heads_second(key, part):
    key = jax.random.fold_in(key, 31)
    return square_draw(key, (LAYERS, D, 3, D), 0.6)


def draw_merge_second(key, part):
    key = jax.random.fold_in(key, 32)
    return square_draw(key, (LAYERS, D, D), 0.95)


def draw_expand_second(key, part):
    key = jax.random.fold_in(key, 33)
    return square_draw(key, (LAYERS, D, 4, D), 0.7)


def draw_shrink_second(key, part):
    key = jax.random.fold_in(key, 34)
    return square_draw(key, (LAYERS, D, 4, D), 0.7)


def draw_shared_second(key, part):
    key = jax.random.fold_in(key, 35)
    return square_draw(key, (LAYERS, 6, D), shared_levels())


def draw_split_second(key, part):
    key = jax.random.fold_in(key, 36)
    return square_draw(key, (LAYERS, 6, D), 0.9)


def draw_shared_vectors(key, part):
    key = jax.random.fold_in(key, 21)
    gain_key = jax.random.fold_in(key, 1)
    bias_key = jax.random.fold_in(key, 2)
    row_index = jnp.arange(6).reshape(1, 6, 1)
    gain_rows = (row_index == 0) | (row_index == 3)
    gains = 1.0 + 0.2 * jax.random.uniform(gain_key, (LAYERS, 6, D), jnp.float32, -1.0, 1.0)
    normal_part = 0.3 * jnp.clip(jax.random.normal(bias_key, (LAYERS, 6, D), jnp.float32), -4.0, 4.0)
    return jnp.where(gain_rows, gains, normal_part)


def draw_split_vectors(key, part):
    key = jax.random.fold_in(key, 22)
    row_index = jnp.arange(6).reshape(1, 6, 1)
    row_scale = jnp.where(row_index == 1, 0.03, 0.3)
    normal_part = jnp.clip(jax.random.normal(key, (LAYERS, 6, D), jnp.float32), -4.0, 4.0)
    return row_scale * normal_part


def steps_of(stream_key, shape, shards, low, largest):
    loudness = 1.0
    for dim, parts in shards:
        steps = jax.random.uniform(jax.random.fold_in(jax.random.fold_in(stream_key, 6), dim), (parts,), jnp.float32, low / len(shards), largest / len(shards))
        loudness = loudness * jnp.repeat(jnp.exp(steps), shape[dim] // parts).reshape((-1,) + (1,) * (len(shape) - 1 - dim))
    return loudness


def normal_values(key, dims, width, limit, pieces=(), kind=jnp.bfloat16):
    entries = jax.random.normal(key, dims, jnp.float32) * width
    if len(pieces) > 0:
        entries = steps_of(key, dims, pieces, -0.22, 0.18) * entries
    return jnp.clip(entries, min=-limit, max=limit).astype(kind)


def setup_inputs(seed: int = 0) -> dict:
    key_of = jax.random.split(jax.random.key(seed), 21)
    frames = normal_values(key_of[0], (CLIPS, FRAMES, D), 1.0, 6.0, ((0, 4), (1, 2)))
    cotangent = normal_values(key_of[1], (CLIPS, FRAMES, D), 1.0, 6.0, ((0, 4), (1, 2)))
    heads_weight = normal_values(key_of[2], (LAYERS, D, 3, D), (4 * D // 9) ** -0.5, 0.3125, ((1, 8), (3, 4)), jnp.float32)
    merge_weight = normal_values(key_of[3], (LAYERS, D, D), D ** -0.5, 0.21875, ((1, 8), (2, 4)), jnp.float32)
    expand_weight = normal_values(key_of[4], (LAYERS, D, 4, D), D ** -0.5, 0.21875, ((1, 8), (3, 4)), jnp.float32)
    shrink_weight = normal_values(key_of[5], (LAYERS, D, 4, D), D ** -0.5, 0.21875, ((1, 8), (3, 4)), jnp.float32)
    shared_vectors = draw_shared_vectors(jax.random.fold_in(key_of[20], 71), 0)
    split_vectors = draw_split_vectors(jax.random.fold_in(key_of[20], 71), 0)
    heads_first = draw_heads_first(jax.random.fold_in(key_of[20], 71), 0)
    heads_second = draw_heads_second(jax.random.fold_in(key_of[20], 71), 0)
    merge_first = draw_merge_first(jax.random.fold_in(key_of[20], 71), 0)
    merge_second = draw_merge_second(jax.random.fold_in(key_of[20], 71), 0)
    expand_first = draw_expand_first(jax.random.fold_in(key_of[20], 71), 0)
    expand_second = draw_expand_second(jax.random.fold_in(key_of[20], 71), 0)
    shrink_first = draw_shrink_first(jax.random.fold_in(key_of[20], 71), 0)
    shrink_second = draw_shrink_second(jax.random.fold_in(key_of[20], 71), 0)
    shared_first = draw_shared_first(jax.random.fold_in(key_of[20], 71), 0)
    shared_second = draw_shared_second(jax.random.fold_in(key_of[20], 71), 0)
    split_first = draw_split_first(jax.random.fold_in(key_of[20], 71), 0)
    split_second = draw_split_second(jax.random.fold_in(key_of[20], 71), 0)
    return dict(frames=frames, cotangent=cotangent, heads_weight=heads_weight, merge_weight=merge_weight, expand_weight=expand_weight, shrink_weight=shrink_weight, shared_vectors=shared_vectors, split_vectors=split_vectors, heads_first=heads_first, heads_second=heads_second, merge_first=merge_first, merge_second=merge_second, expand_first=expand_first, expand_second=expand_second, shrink_first=shrink_first, shrink_second=shrink_second, shared_first=shared_first, shared_second=shared_second, split_first=split_first, split_second=split_second)


beta_one = 0.9
beta_two = 0.999
adam_epsilon = 1e-08
weight_decay = 0.01
norm_epsilon = 1e-05
highest_precision = lax.Precision.HIGHEST

@jax.custom_vjp
def low(v):
    return lax.optimization_barrier(v.astype(jnp.bfloat16)).astype(jnp.float32)

@jax.custom_vjp
def low_back(v):
    return v

def low_keep(v):
    return (low(v), None)

def low_pass(kept, grad):
    return (grad,)

def back_keep(v):
    return (v, None)

def back_low(kept, grad):
    return (low(grad),)
low.defvjp(low_keep, low_pass)
low_back.defvjp(back_keep, back_low)

def layer_norm(values, gain_row, shift_row):
    centre = values - lax.optimization_barrier(jnp.mean(values, axis=-1, keepdims=True))
    spread = lax.optimization_barrier(jnp.mean(centre * centre, axis=-1, keepdims=True))
    return centre * lax.rsqrt(spread + norm_epsilon) * gain_row + shift_row

def encoder_layer(stream, heads_full, merge_full, expand_full, shrink_full, shared, split_rows):
    scaling = HEAD_DIM ** (-0.5)
    normed = low(layer_norm(stream, shared[0], shared[1]))
    project = jnp.einsum('td,dke->tke', normed, heads_full, precision=highest_precision)
    query_rows = low(low_back(project[:, 0] + split_rows[0]))
    key_rows = low(low_back(project[:, 1]))
    value_rows = low(low_back(project[:, 2] + split_rows[1]))
    query_heads = query_rows.reshape(FRAMES, HEADS, HEAD_DIM)
    key_heads = key_rows.reshape(FRAMES, HEADS, HEAD_DIM)
    value_heads = value_rows.reshape(FRAMES, HEADS, HEAD_DIM)
    scores = low_back(jnp.einsum('qhc,khc->hqk', query_heads, key_heads, precision=highest_precision) * scaling)
    shares = low(jax.nn.softmax(scores, axis=-1))
    context = jnp.einsum('hqk,khc->qhc', shares, value_heads, precision=highest_precision).reshape(FRAMES, D)
    context = low(low_back(context))
    attended = low_back(jnp.einsum('te,oe->to', context, merge_full, precision=highest_precision))
    middle = stream + attended + shared[2]
    normed_two = low(layer_norm(middle, shared[3], shared[4]))
    preact = jnp.einsum('td,df->tf', normed_two, expand_full, precision=highest_precision)
    preact = low_back(preact + split_rows[2:].reshape(FF))
    hidden = low(jax.nn.gelu(preact, approximate=False))
    output = low_back(jnp.einsum('tf,of->to', hidden, shrink_full, precision=highest_precision))
    return middle + output + shared[5]

def adam_update(weight, gradient, first_moment, second, step_rate):
    first_new = beta_one * first_moment + (1.0 - beta_one) * gradient
    second_new = beta_two * second + (1.0 - beta_two) * gradient * gradient
    bias_one = 1.0 - beta_one ** STEP
    bias_two = 1.0 - beta_two ** STEP
    direction = first_new / bias_one / (jnp.sqrt(second_new / bias_two) + adam_epsilon)
    return (second_new, weight - step_rate * (direction + weight_decay * weight))

def reference(frames, cotangent, heads_weight, merge_weight, expand_weight, shrink_weight, shared_vectors, split_vectors, heads_first, heads_second, merge_first, merge_second, expand_first, expand_second, shrink_first, shrink_second, shared_first, shared_second, split_first, split_second):

    def forward(params, inputs):
        heads_all, merge_all, expand_all, shrink_all, shared_all, split_all = params
        heads_low = low(heads_all)
        merge_low = low(merge_all)
        expand_low = low(expand_all)
        shrink_low = low(shrink_all)

        def one_clip(stream):
            for layer_index in range(LAYERS):
                stream = encoder_layer(stream, heads_low[layer_index], merge_low[layer_index], expand_low[layer_index].reshape(D, FF), shrink_low[layer_index].reshape(D, FF), shared_all[layer_index], split_all[layer_index])
            return stream
        return lax.map(jax.checkpoint(one_clip), inputs)
    params = (heads_weight, merge_weight, expand_weight, shrink_weight, shared_vectors, split_vectors)
    encoded, pullback = jax.vjp(forward, params, frames.astype(jnp.float32))
    gradients, input_grad = pullback(cotangent.astype(jnp.float32))
    heads_grad, merge_grad, expand_grad, shrink_grad, shared_grad, split_grad = gradients
    heads_renewed, heads_updated = adam_update(heads_weight, heads_grad, heads_first, heads_second, 0.1)
    merge_renewed, merge_updated = adam_update(merge_weight, merge_grad, merge_first, merge_second, 0.1)
    expand_renewed, expand_updated = adam_update(expand_weight, expand_grad, expand_first, expand_second, 0.1)
    shrink_renewed, shrink_updated = adam_update(shrink_weight, shrink_grad, shrink_first, shrink_second, 0.1)
    shared_renewed, shared_updated = adam_update(shared_vectors, shared_grad, shared_first, shared_second, 2.0)
    split_renewed, split_updated = adam_update(split_vectors, split_grad, split_first, split_second, 0.5)
    return (encoded, input_grad, heads_grad, heads_renewed, heads_updated, merge_grad, merge_renewed, merge_updated, expand_grad, expand_renewed, expand_updated, shrink_grad, shrink_renewed, shrink_updated, shared_grad, shared_renewed, shared_updated, split_grad, split_renewed, split_updated)
```

```python
import math

import jax
import jax.numpy as jnp
from jax import lax
from jax.experimental import pallas as pl
from jax.experimental.pallas import tpu as pltpu
from jax.sharding import PartitionSpec as P

HEAD_DIM = 64
STEP = 10

beta_one = 0.9
beta_two = 0.999
adam_epsilon = 1e-08
weight_decay = 0.01
norm_epsilon = 1e-05

MESH = pl.DeviceIdType.MESH
F32 = jnp.float32
BF16 = jnp.bfloat16


def dot(a, b):
    return lax.dot_general(a, b, (((1,), (0,)), ((), ())), preferred_element_type=F32)


def dot_nt(a, b):
    return lax.dot_general(a, b, (((1,), (1,)), ((), ())), preferred_element_type=F32)


def dot_tn(a, b):
    return lax.dot_general(a, b, (((0,), (0,)), ((), ())), preferred_element_type=F32)


def norm_parts(values):
    centre = values - jnp.mean(values, axis=-1, keepdims=True)
    spread = jnp.mean(centre * centre, axis=-1, keepdims=True)
    inverse = lax.rsqrt(spread + norm_epsilon)
    return centre * inverse, inverse


def norm_back(grad, hat, inverse, gain):
    scaled = grad * gain
    first = jnp.mean(scaled, axis=-1, keepdims=True)
    second = jnp.mean(scaled * hat, axis=-1, keepdims=True)
    return inverse * (scaled - first - hat * second)


class Numbers:
    def __init__(self):
        self.count = 0

    def take(self, n):
        base = self.count
        self.count += n
        return base


def make_kernel(layers, tokens, width, numbers):
    shard = tokens // 4
    rows_of = 96
    take = numbers.take
    rs_base = [take(3) for _ in range(3 * layers)]
    ag_base = [take(4) for _ in range(4 * layers)]
    sp_base = [take(16), take(16)]
    sv_base, sz_base, sc_base, sq_base = take(3), take(3), take(1), take(3)
    cx_base = [take(3) for _ in range(layers)]
    gc_base = [take(3) for _ in range(layers)]
    ob, oa, oc = ([take(n) for _ in range(layers)] for n in (3, 3, 4))
    goc, goa, gob = ([take(n) for _ in range(layers)] for n in (1, 3, 3))
    kv_base = [take(2) for _ in range(layers)]
    gkv_base = [take(1) for _ in range(layers)]
    ab, aa, ac = ([take(n) for _ in range(layers)] for n in (4, 3, 4))
    ma, mb, mc = ([take(n) for _ in range(layers)] for n in (3, 4, 4))
    gac, gaa, gab = ([take(n) for _ in range(layers)] for n in (1, 3, 4))
    gmc, gmb, gma = ([take(n) for _ in range(layers)] for n in (1, 4, 3))
    oz = [take(4) for _ in range(2)]
    op = [take(4) for _ in range(2)]
    top = layers - 1

    def kernel(
        frames, cot, hw, mw, wm, shared, sv,
        enc, xg, gh_out, go_out, gm_out, shared_out, split_out,
        XS, MS, A, N, GO, GY, GS,
        WA, WO, W1, W2, GA, GB, GM,
        QC, KV, VT, E01, E2, RR, CS, CX, CF, GC, H, DG, GF, GQ, G,
        GKV, KVS, KVR,
        OWN, RSS, RSR,
        CM, BM, TM, UM,
        FM, FA, SA, CA, RA, RB, SO, CO, RO, TO, RP,
        EZ, SV, BQ, B1, SMALL, SZ, SC, SP,
        ssem, rsem, lsem,
    ):
        dp = lax.axis_index("dp")
        y = lax.axis_index("seq")
        z = lax.axis_index("tensor")
        hi = lax.div(dp, 4)
        lo = lax.rem(dp, 4)
        xx = lax.div(lo, 2)
        cc = lax.rem(lo, 2)
        t = 2 * xx + y

        def flip(bit, by):
            return bit + by - 2 * bit * by

        def peer(k):
            if isinstance(k, int):
                kx, ky = k // 2, k % 2
            else:
                kx, ky = lax.div(k, 2), lax.rem(k, 2)
            return flip(xx, kx), flip(y, ky)

        def peer_t(k):
            px, py = peer(k)
            return 2 * px + py

        def peer_dev(k):
            px, py = peer(k)
            return {"dp": 4 * hi + 2 * px + cc, "seq": py}

        def peer_j(k):
            px, py = peer(k)
            return 4 * px + 2 * cc + py

        my_j = 4 * xx + 2 * cc + y
        sib = {"dp": dp + 1 - 2 * cc}

        def z_to(k):
            return lax.rem(z + k, 4)

        def z_from(k):
            return lax.rem(z + 4 - k, 4)

        middle = jnp.logical_or(z == 1, z == 2)

        def z_near(k, act):
            if k == 2:
                act()
            else:
                pl.when(z != (3 if k == 1 else 0))(act)

        def z_far(k, act):
            pl.when(z == (3 if k == 1 else 0))(act)

        def z_come(k, act):
            pl.when(z != (0 if k == 1 else 3))(act)

        def gather_z(slot, base):
            def copy(k):
                return remote(slot(z), slot(z), base + k - 1, {"tensor": z_to(k)})

            def relay():
                far = slot(z_from(2))
                return remote(
                    far, far, base + 2 * (z - 1), {"tensor": 3 * (z - 1)}, send=base + 3
                )

            def wait(k):
                remote(slot(z), slot(z_from(k)), base + k - 1, sib).wait_recv()

            def start():
                for k in (2, 1, 3):
                    z_near(k, lambda k=k: copy(k).start())

            def pass_on():
                wait(2)
                pl.when(middle)(lambda: relay().start())

            def drain():
                for k in (2, 1, 3):
                    z_near(k, lambda k=k: copy(k).wait_send())
                pl.when(middle)(lambda: relay().wait_send())

            return start, pass_on, wait, drain

        def sum_z(part, far, landing, base):
            def copy(k):
                return remote(part(z_to(k)), landing(k), base + k - 1, {"tensor": z_to(k)})

            def far_copy():
                end = lax.div(z, 3)
                return remote(part(3 - z), far, base + 3, {"tensor": 1 + end})

            def start_far():
                pl.when(jnp.logical_not(middle))(lambda: far_copy().start())

            def start():
                for k in (1, 3):
                    z_near(k, lambda k=k: copy(k).start())
                    at = landing(k)

                    @pl.when(z == (0 if k == 1 else 3))
                    def _(at=at):
                        at[...] = jnp.zeros(at.shape, BF16)

                pl.when(jnp.logical_not(middle))(lambda: copy(2).start())

            def combine():
                @pl.when(middle)
                def _():
                    far_copy().wait_recv()
                    at = part(z_to(2))
                    at[...] = (at[...].astype(F32) + far[...].astype(F32)).astype(BF16)
                    copy(2).start()

            def wait():
                copy(2).wait_recv()
                for k in (1, 3):
                    z_come(k, lambda k=k: copy(k).wait_recv())

            def drain():
                copy(2).wait_send()
                for k in (1, 3):
                    z_near(k, lambda k=k: copy(k).wait_send())
                pl.when(jnp.logical_not(middle))(lambda: far_copy().wait_send())

            return start, combine, wait, drain, start_far

        def remote(src, dst, number, dev, send=None):
            send = number if send is None else send
            return pltpu.make_async_remote_copy(
                src_ref=src,
                dst_ref=dst,
                send_sem=ssem.at[send],
                recv_sem=rsem.at[number],
                device_id=dev,
                device_id_type=MESH,
            )

        def rows(k_t):
            return pl.ds(pl.multiple_of(k_t * shard, shard), shard)

        def block(j):
            return pl.ds(pl.multiple_of(j * rows_of, rows_of), rows_of)

        X0 = GF
        lower = lax.broadcasted_iota(jnp.int32, (1, 128), 1) < 64
        top_rows = lax.broadcasted_iota(jnp.int32, (128, 1), 0) < 64

        barrier = pltpu.get_barrier_semaphore()
        for k in range(1, 8):
            dev = {
                "dp": 4 * hi + 2 * flip(xx, k // 4) + flip(cc, (k // 2) % 2),
                "seq": flip(y, k % 2),
            }
            pl.semaphore_signal(barrier, inc=1, device_id=dev, device_id_type=MESH)
        for k in range(1, 4):
            pl.semaphore_signal(
                barrier, inc=1, device_id={"tensor": z_to(k)}, device_id_type=MESH
            )
        pl.semaphore_wait(barrier, 10)

        xs = lax.div(z, 2)
        source = jnp.logical_and(lo == z, y == cc)
        relay = jnp.logical_and(xx != xs, y == cc)
        relay_dev = {"dp": dp, "seq": 1 - y}

        def piece(p):
            return pl.ds(p * shard, shard)

        def spread_each(src, dst, i, act, act_own):
            @pl.when(lo == z)
            def _():
                for p in range(4):
                    for d, (dx, dy) in enumerate(((1, 0), (0, 1), (0, 0))):
                        same = jnp.logical_and(cc == y, (dx, dy) == (0, 0))
                        dev = {"dp": 4 * hi + 2 * flip(xx, dx) + y, "seq": flip(y, dy)}

                        @pl.when(jnp.logical_not(same))
                        def _(p=p, d=d, dev=dev):
                            act(
                                remote(
                                    src.at[piece(p)],
                                    dst.at[piece(p)],
                                    sp_base[i] + p,
                                    dev,
                                    send=sp_base[i] + 4 + 3 * p + d,
                                )
                            )

            if act_own is not None:

                @pl.when(source)
                def _():
                    act_own(pltpu.make_async_copy(src, dst, lsem.at[i]))

        def spread_start(src, dst, i):
            spread_each(src, dst, i, lambda c: c.start(), lambda c: c.start())

        def relay_copy(dst, i, p):
            return remote(
                dst.at[piece(p)],
                dst.at[piece(p)],
                sp_base[i] + p,
                relay_dev,
                send=sp_base[i] + 4 + p,
            )

        def spread_pass(dst, i, p):
            @pl.when(relay)
            def _():
                relay_copy(dst, i, p).wait_recv()
                relay_copy(dst, i, p).start()

        def spread_wait(src, dst, i, p):
            if p == 0:

                @pl.when(source)
                def _():
                    pltpu.make_async_copy(src, dst, lsem.at[i]).wait()

            @pl.when(jnp.logical_not(jnp.logical_or(source, relay)))
            def _():
                relay_copy(dst, i, p).wait_recv()

        def spread_drain(src, dst, i):
            spread_each(src, dst, i, lambda c: c.wait_send(), None)

            @pl.when(relay)
            def _():
                for p in range(4):
                    relay_copy(dst, i, p).wait_send()

        att_z = [gather_z(lambda b, l=l: GA.at[l, b], ab[l]) for l in range(layers)]
        mlp_z = [gather_z(lambda b, l=l: GM.at[l, cc, b], mb[l]) for l in range(layers)]
        out_z = [gather_z(lambda b, i=i: EZ.at[i, b], oz[i]) for i in range(2)]

        def att_b_start(l):
            q, k, v = (hw[l, i].astype(BF16) for i in range(3))
            GA[l, z, :, 0:128] = q[:, 0:128]
            GA[l, z, :, 128:256] = jnp.concatenate([q[:, 128:192], k[:, 128:192]], axis=1)
            GA[l, z, :, 256:384] = k[:, 0:128]
            GA[l, z, :, 384:512] = v[:, 0:128]
            third = v[:, 128:192]
            GA[l, z, :, 512:640] = jnp.concatenate([third, jnp.zeros_like(third)], axis=1)
            att_z[l][0]()

        def att_a_copy(l, b):
            bx, by = lax.div(b, 2), lax.rem(b, 2)
            k = 2 * flip(xx, bx) + flip(y, by)
            return remote(
                GA.at[l, b],
                WA.at[l, block(my_j)],
                aa[l] + k - 1,
                {"dp": 4 * hi + 2 * bx + cc, "seq": by},
            )

        def att_a_piece(l, zk):
            b = z_from(zk)

            @pl.when(b != t)
            def _():
                att_a_copy(l, b).start()

            @pl.when(b == t)
            def _():
                WA[l, block(my_j)] = GA[l, t]

        def att_a_first(l):
            att_z[l][1]()
            att_a_piece(l, 2)

        def att_a_rest(l):
            for k in (1, 3):
                att_z[l][2](k)
                att_a_piece(l, k)

        def att_c_copy(l, k):
            at = WA.at[l, block(peer_j(k))]
            return remote(at, at, ac[l] + k, sib)

        def att_c_start(l):
            att_c_copy(l, 0).start()
            for k in range(1, 4):
                remote(
                    GA.at[l, 0], WA.at[l, block(peer_j(k))], aa[l] + k - 1, sib
                ).wait_recv()
                att_c_copy(l, k).start()

        def att_ready(l):
            for k in range(4):
                px, py = peer(k)
                at = WA.at[l, block(4 * px + 2 * (1 - cc) + py)]
                remote(at, at, ac[l] + k, sib).wait_recv()

        def att_drain(l):
            att_z[l][3]()
            for k in range(1, 4):
                att_a_copy(l, peer_t(k)).wait_send()
            for k in range(4):
                att_c_copy(l, k).wait_send()

        def out_b_copy(l, k):
            return remote(GB.at[l, z], GB.at[l, z], ob[l] + k - 1, {"tensor": z_to(k)})

        def out_b_start(l):
            own = mw[l].astype(BF16)
            third = own[:, 128:192]
            none = jnp.zeros_like(third)
            odd = lax.rem(z, 2) == 1
            GB[l, z, :, 0:128] = own[:, 0:128]
            GB[l, z, :, 128:256] = jnp.where(
                odd,
                jnp.concatenate([none, third], axis=1),
                jnp.concatenate([third, none], axis=1),
            )
            for k in range(1, 4):
                out_b_copy(l, k).start()

        def out_a_copy(l, k):
            at = WO.at[l, block(my_j)]
            return remote(at, at, oa[l] + k - 1, peer_dev(k))

        def out_a_start(l):
            for k in range(1, 4):
                remote(GB.at[l, z], GB.at[l, z_from(k)], ob[l] + k - 1, sib).wait_recv()
            at = block(my_j)
            for b in range(4):
                WO[l, at, b * 128 : b * 128 + 128] = GB[l, b, :, 0:128]
            for b in range(2):
                pair = GB[l, 2 * b, :, 128:256] + GB[l, 2 * b + 1, :, 128:256]
                WO[l, at, 512 + b * 128 : 640 + b * 128] = pair
            for k in range(1, 4):
                out_a_copy(l, k).start()

        def out_c_copy(l, k):
            at = WO.at[l, block(peer_j(k))]
            return remote(at, at, oc[l] + k, sib)

        def out_c_start(l):
            out_c_copy(l, 0).start()
            for k in range(1, 4):
                at = WO.at[l, block(peer_j(k))]
                remote(at, at, oa[l] + k - 1, sib).wait_recv()
                out_c_copy(l, k).start()

        def out_ready(l):
            for k in range(4):
                px, py = peer(k)
                at = WO.at[l, block(4 * px + 2 * (1 - cc) + py)]
                remote(at, at, oc[l] + k, sib).wait_recv()

        def out_drain(l):
            for k in range(1, 4):
                out_b_copy(l, k).wait_send()
                out_a_copy(l, k).wait_send()
            for k in range(4):
                out_c_copy(l, k).wait_send()

        def mlp_a_copy(l, k):
            return remote(
                wm.at[l, peer_t(k)], GM.at[l, cc, z, t], ma[l] + k - 1, peer_dev(k)
            )

        def mlp_a_start(l):
            for k in range(1, 4):
                mlp_a_copy(l, k).start()
            GM[l, cc, z, t] = wm[l, t]

        def mlp_b_start(l):
            for k in range(1, 4):
                remote(
                    wm.at[l, 0], GM.at[l, cc, z, peer_t(k)], ma[l] + k - 1, sib
                ).wait_recv()
            mlp_z[l][0]()

        def mlp_pass(l):
            mlp_z[l][1]()

        def mlp_c_copy(l, k):
            at = GM.at[l, cc, z_from(k)]
            return remote(at, at, mc[l] + k, sib)

        def mlp_c_start(l):
            mlp_c_copy(l, 0).start()
            mlp_c_copy(l, 2).start()
            for k in (1, 3):
                mlp_z[l][2](k)
                mlp_c_copy(l, k).start()

        def mlp_ready(l):
            for k in range(4):
                at = GM.at[l, 1 - cc, z_from(k)]
                remote(at, at, mc[l] + k, sib).wait_recv()
            for k in range(4):
                mlp_c_copy(l, k).wait_send()
            for k in range(1, 4):
                mlp_a_copy(l, k).wait_send()
            mlp_z[l][3]()

            def unpack(j, carry):
                jc = lax.rem(lax.div(j, 2), 2)
                jq = 2 * lax.div(j, 4) + lax.rem(j, 2)
                at = block(j)
                mixed = []
                for b in range(4):
                    chunk = GM[l, jc, b, jq]
                    W1[l, at, b * 128 : b * 128 + 128] = chunk[:, 0:128]
                    W2[l, at, b * 128 : b * 128 + 128] = chunk[:, 256:384]
                    mixed.append(chunk[:, 128:256].astype(F32))
                for b in range(2):
                    even, odd = mixed[2 * b], mixed[2 * b + 1]
                    lanes = slice(512 + b * 128, 640 + b * 128)
                    W1[l, at, lanes] = jnp.where(
                        lower, even, pltpu.roll(odd, 64, 1)
                    ).astype(BF16)
                    W2[l, at, lanes] = jnp.where(
                        lower, pltpu.roll(even, 64, 1), odd
                    ).astype(BF16)
                return carry

            lax.fori_loop(0, 8, unpack, 0)

        def rs_copy(i, k):
            return remote(RSS.at[k], RSR.at[i % 2, k - 1], rs_base[i] + k - 1, peer_dev(k))

        def rs_loop(i, order, part):
            def step(s, carry):
                k = order(s)
                partial = part(k)
                RSS[k] = partial.astype(BF16)

                @pl.when(k == 0)
                def _():
                    OWN[...] = partial

                @pl.when(k > 0)
                def _():
                    rs_copy(i, k).start()

                return carry

            lax.fori_loop(0, 4, step, 0)

        def rs_finish(i):
            for k in range(1, 4):
                rs_copy(i, k).wait_recv()
            total = OWN[...]
            for k in range(1, 4):
                total = total + RSR[i % 2, k - 1].astype(F32)
            for k in range(1, 4):
                rs_copy(i, k).wait_send()
            return total

        def ag_copy(i, buf, l, k):
            at = buf.at[l, rows(t)]
            return remote(at, at, ag_base[i] + k - 1, peer_dev(k))

        def ag_half(buf, l, k, upper):
            start = peer_t(k) * shard + upper * (shard // 2)
            return buf.at[l, pl.ds(pl.multiple_of(start, shard // 2), shard // 2)]

        def ag_relay(i, buf, l, k):
            at = ag_half(buf, l, k, k - 1)
            return remote(at, at, ag_base[i] + k + 1, peer_dev(3 - k))

        def ag_start(i, buf, l, value):
            buf[l, rows(t)] = value
            for k in (1, 2):
                ag_copy(i, buf, l, k).start()

        def ag_wait(i, buf, l, k):
            @pl.when(k == 1)
            def _():
                for near in (1, 2):
                    at = buf.at[l, rows(peer_t(near))]
                    remote(at, at, ag_base[i] + near - 1, sib).wait_recv()
                    ag_relay(i, buf, l, near).start()

            @pl.when(k == 3)
            def _():
                for upper in (0, 1):
                    at = ag_half(buf, l, 3, upper)
                    remote(at, at, ag_base[i] + 2 + upper, sib).wait_recv()

        def ag_drain(i, buf, l):
            for k in (1, 2):
                ag_copy(i, buf, l, k).wait_send()
                ag_relay(i, buf, l, k).wait_send()

        def forth(s):
            return s

        def back(s):
            return 3 - s

        def row(l, r):
            return shared[r, l : l + 1, :]

        def out_start(i, value):
            EZ[i, z] = value.astype(BF16)
            out_z[i][0]()

        def out_p_each(i, ks, act_far, act_near):
            for k in ks:
                zs = z_from(k)
                near = jnp.logical_and(lo == zs, y == cc)

                @pl.when(near)
                def _(zs=zs):
                    act_near(
                        pltpu.make_async_copy(
                            EZ.at[i, zs], (enc, xg)[i].at[t], lsem.at[2 + i]
                        )
                    )

                @pl.when(jnp.logical_not(near))
                def _(zs=zs, k=k):
                    act_far(
                        remote(
                            EZ.at[i, zs],
                            (enc, xg)[i].at[t],
                            op[i] + t,
                            {"dp": 4 * hi + zs, "seq": cc},
                            send=op[i] + k,
                        )
                    )

        def out_forward(i, ks):
            for k in ks:
                if k % 2 == 1:
                    out_z[i][2](k)
                out_p_each(i, (k,), lambda c: c.start(), lambda c: c.start())

        def out_finish(i, out):
            for d in range(4):
                mine = jnp.logical_and(t == d, cc == y)

                @pl.when(jnp.logical_not(mine))
                def _(d=d):
                    remote(EZ.at[i, 0], out.at[d], op[i] + d, sib).wait_recv()

            out_p_each(i, range(4), lambda c: c.wait_send(), lambda c: c.wait())
            out_z[i][3]()

        def att_grad_c_copy(l):
            return remote(SA.at[1 - cc], CA, gac[l], sib)

        def att_grad_a_copy(l, k):
            return remote(
                SA.at[cc, peer_t(k)], RA.at[l, t], gaa[l] + k - 1, peer_dev(k)
            )

        att_sum = [
            sum_z(lambda b, l=l: RA.at[l, b], FA.at[l], lambda k, l=l: RB.at[l, k - 1], gab[l])
            for l in range(layers)
        ]
        mlp_sum = [
            sum_z(lambda b, l=l: GM.at[l, cc, b], FM.at[l], lambda k, l=l: BM.at[l, k - 1], gmb[l])
            for l in range(layers)
        ]

        def att_grad_a(l):
            att_grad_c_copy(l).wait_recv()

            def add(q, carry):
                SA[cc, q] = (
                    SA[cc, q].astype(F32) + CA[q].astype(F32)
                ).astype(BF16)
                return carry

            lax.fori_loop(0, 4, add, 0)
            for k in range(1, 4):
                att_grad_a_copy(l, k).start()
            RA[l, t] = SA[cc, t]
            att_grad_c_copy(l).wait_send()

        def att_grad_b(l):
            for k in range(1, 4):
                remote(
                    SA.at[0, 0], RA.at[l, peer_t(k)], gaa[l] + k - 1, sib
                ).wait_recv()
            att_sum[l][4]()
            att_sum[l][0]()
            for k in range(1, 4):
                att_grad_a_copy(l, k).wait_send()

        def att_grad_end(l):
            total = RA[l, z].astype(F32)
            att_sum[l][2]()
            for k in range(1, 4):
                total = total + RB[l, k - 1].astype(F32)
            gh_out[l, 0, :, :] = total[:, 0:192].astype(BF16)
            gh_out[l, 1, :, 0:128] = total[:, 256:384].astype(BF16)
            k2 = pltpu.roll(total[:, 128:256], 64, 1)[:, 0:64]
            gh_out[l, 1, :, 128:192] = k2.astype(BF16)
            gh_out[l, 2, :, :] = total[:, 384:576].astype(BF16)
            att_sum[l][3]()

        def out_grad_c_copy(l):
            return remote(SO.at[1 - cc], CO, goc[l], sib)

        def out_grad_a_copy(l, k):
            return remote(SO.at[cc, peer_t(k)], RO.at[l, k - 1], goa[l] + k - 1, peer_dev(k))

        def out_grad_b_copy(l, k):
            return remote(
                TO.at[z_to(k)], RP.at[l, k - 1], gob[l] + k - 1, {"tensor": z_to(k)}
            )

        def out_grads(l):
            def product(b, carry):
                lanes = pl.ds(pl.multiple_of(b * 128, 128), 128)
                W2[l, lanes, :] = dot_tn(GO[l, :, lanes], CF[l]).astype(BF16)
                return carry

            lax.fori_loop(0, 6, product, 0)

            def pack(j, carry):
                jc = lax.rem(lax.div(j, 2), 2)
                jq = 2 * lax.div(j, 4) + lax.rem(j, 2)
                SO[jc, jq] = W2[l, block(j), :]
                return carry

            lax.fori_loop(0, 8, pack, 0)
            out_grad_c_copy(l).start()

        def out_grad_a(l):
            out_grad_c_copy(l).wait_recv()

            def add(q, carry):
                SO[cc, q] = (SO[cc, q].astype(F32) + CO[q].astype(F32)).astype(BF16)
                return carry

            lax.fori_loop(0, 4, add, 0)
            for k in range(1, 4):
                out_grad_a_copy(l, k).start()
            out_grad_c_copy(l).wait_send()

        def out_grad_b(l):
            total = SO[cc, t].astype(F32)
            for k in range(1, 4):
                out_grad_a_copy(l, k).wait_recv()
                total = total + RO[l, k - 1].astype(F32)
            total = total.astype(BF16)
            for b in range(4):
                TO[b, :, 0:128] = total[:, b * 128 : b * 128 + 128]
                pair = 512 + (b // 2) * 128
                TO[b, :, 128:256] = total[:, pair : pair + 128]
            for k in range(1, 4):
                out_grad_b_copy(l, k).start()
            for k in range(1, 4):
                out_grad_a_copy(l, k).wait_send()

        def out_grad_end(l):
            total = TO[z].astype(F32)
            for k in range(1, 4):
                out_grad_b_copy(l, k).wait_recv()
                total = total + RP[l, k - 1].astype(F32)
            go_out[l, :, 0:128] = total[:, 0:128].astype(BF16)
            pair = total[:, 128:256]
            pair = jnp.where(lax.rem(z, 2) == 1, pltpu.roll(pair, 64, 1), pair)
            go_out[l, :, 128:192] = pair[:, 0:64].astype(BF16)
            for k in range(1, 4):
                out_grad_b_copy(l, k).wait_send()

        def mlp_grad_c_copy(l):
            return remote(GM.at[l, 1 - cc], CM, gmc[l], sib)

        def mlp_grad_a_copy(l, k):
            return remote(TM.at[peer_t(k)], UM.at[l, t], gma[l] + k - 1, peer_dev(k))

        def mlp_grad_b(l):
            mlp_grad_c_copy(l).wait_recv()

            def add(s, carry):
                zs, q = lax.div(s, 4), lax.rem(s, 4)
                GM[l, cc, zs, q] = (
                    GM[l, cc, zs, q].astype(F32) + CM[zs, q].astype(F32)
                ).astype(BF16)
                return carry

            lax.fori_loop(0, 16, add, 0)
            mlp_sum[l][4]()
            mlp_grad_c_copy(l).wait_send()

        def mlp_grad_a(l):
            mlp_sum[l][2]()
            for q in range(4):
                total = GM[l, cc, z, q].astype(F32)
                for k in range(1, 4):
                    total = total + BM[l, k - 1, q].astype(F32)
                TM[q] = total.astype(BF16)
            for k in range(1, 4):
                mlp_grad_a_copy(l, k).start()
            UM[l, t] = TM[t]

        def mlp_grad_end(l):
            for k in range(1, 4):
                remote(TM.at[0], UM.at[l, peer_t(k)], gma[l] + k - 1, sib).wait_recv()
            gm_out[l] = UM[l]
            for k in range(1, 4):
                mlp_grad_a_copy(l, k).wait_send()
            mlp_sum[l][3]()

        def mlp_grads(l):
            def product(b, carry):
                lanes = pl.ds(pl.multiple_of(b * 128, 128), 128)
                W2[l, lanes, :] = dot_tn(GY[l, :, lanes], H[l]).astype(BF16)
                W1[l, lanes, :] = dot_tn(N[l, :, lanes], GF[...]).astype(BF16)
                return carry

            lax.fori_loop(0, 6, product, 0)

            def pack(j, carry):
                jc = lax.rem(lax.div(j, 2), 2)
                jq = 2 * lax.div(j, 4) + lax.rem(j, 2)
                at = block(j)
                for b in range(4):
                    lanes = slice(b * 128, b * 128 + 128)
                    GM[l, jc, b, jq, :, 0:128] = W1[l, at, lanes]
                    GM[l, jc, b, jq, :, 256:384] = W2[l, at, lanes]
                for b in range(2):
                    lanes = slice(512 + b * 128, 640 + b * 128)
                    one, two = W1[l, at, lanes].astype(F32), W2[l, at, lanes].astype(F32)
                    GM[l, jc, 2 * b, jq, :, 128:256] = jnp.where(
                        lower, one, pltpu.roll(two, 64, 1)
                    ).astype(BF16)
                    GM[l, jc, 2 * b + 1, jq, :, 128:256] = jnp.where(
                        lower, pltpu.roll(one, 64, 1), two
                    ).astype(BF16)
                return carry

            lax.fori_loop(0, 8, pack, 0)
            mlp_grad_c_copy(l).start()
            SMALL[8 * l + 7 : 8 * l + 8, :] = jnp.sum(GF[...].astype(F32), axis=0, keepdims=True)

        def att_grads(l):
            def product(b, carry):
                lanes = pl.ds(pl.multiple_of(b * 128, 128), 128)
                W1[l, lanes, 0:640] = dot_tn(A[l, :, lanes], G[...]).astype(BF16)
                return carry

            lax.fori_loop(0, 6, product, 0)

            def pack(j, carry):
                jc = lax.rem(lax.div(j, 2), 2)
                jq = 2 * lax.div(j, 4) + lax.rem(j, 2)
                SA[jc, jq] = W1[l, block(j), 0:640]
                return carry

            lax.fori_loop(0, 8, pack, 0)
            att_grad_c_copy(l).start()
            SMALL[8 * l + 6 : 8 * l + 7, 0:640] = jnp.sum(G[...].astype(F32), axis=0, keepdims=True)
            SMALL[8 * l + 6 : 8 * l + 7, 640:768] = jnp.zeros((1, 128), F32)

        def sv_copy(k):
            return remote(SV.at[z], SV.at[z], sv_base + k - 1, {"tensor": z_to(k)})

        def biases_start():
            SV[z] = jnp.zeros((layers, 8, 256), F32)
            for l in range(layers):
                for r in range(6):
                    SV[z, l, r : r + 1, 0:192] = sv[r, l : l + 1, :]
            for k in range(1, 4):
                sv_copy(k).start()

        def biases_ready():
            for k in range(1, 4):
                remote(SV.at[z], SV.at[z_from(k)], sv_base + k - 1, sib).wait_recv()
            for l in range(layers):
                BQ[l, :, 0:256] = SV[t, l, 0:1, :]
                BQ[l, :, 256:384] = jnp.zeros((1, 128), F32)
                BQ[l, :, 384:640] = SV[t, l, 1:2, :]
                hidden = [SV[b, l, pl.ds(2 + t, 1), :] for b in range(4)]
                for b in range(4):
                    B1[l, :, b * 128 : b * 128 + 128] = hidden[b][:, 0:128]
                for b in range(2):
                    even, odd = hidden[2 * b][:, 128:256], hidden[2 * b + 1][:, 128:256]
                    B1[l, :, 512 + b * 128 : 640 + b * 128] = jnp.where(
                        lower, even, pltpu.roll(odd, 64, 1)
                    )
            for k in range(1, 4):
                sv_copy(k).wait_send()

        def sz_copy(k):
            return remote(SMALL, SZ.at[k - 1], sz_base + k - 1, {"tensor": z_to(k)})

        def sc_copy():
            return remote(SZ.at[0], SC, sc_base, sib)

        def sq_copy(k):
            return remote(SP.at[t], SP.at[t], sq_base + k - 1, peer_dev(k))

        def small_z():
            for k in range(1, 4):
                sz_copy(k).start()

        def small_c():
            for k in range(1, 4):
                sz_copy(k).wait_recv()
            SZ[0] = SMALL[...] + SZ[0] + SZ[1] + SZ[2]
            sc_copy().start()

        def small_q():
            sc_copy().wait_recv()
            SP[t] = SZ[0] + SC[...]
            for k in range(1, 4):
                sq_copy(k).start()

        def small_end():
            for k in range(1, 4):
                remote(SC, SP.at[peer_t(k)], sq_base + k - 1, sib).wait_recv()
            z_half = lax.div(z, 2)
            upper = lax.rem(z, 2)
            for l in range(layers):
                at = slice(8 * l, 8 * l + 6)
                total = SP[0, at] + SP[1, at] + SP[2, at] + SP[3, at]
                for r in range(6):
                    shared_out[r, l : l + 1, :] = total[r : r + 1]
                line = slice(8 * l + 6, 8 * l + 7)
                split_out[0, l : l + 1, :] = SP[z, line, 0:192]
                split_out[1, l : l + 1, :] = SP[z, line, 384:576]
                line = slice(8 * l + 7, 8 * l + 8)
                for r in range(4):
                    first = SP[r, line, pl.ds(pl.multiple_of(z * 128, 128), 128)]
                    pair = SP[
                        r, line, pl.ds(pl.multiple_of(512 + z_half * 128, 128), 128)
                    ]
                    pair = jnp.where(upper == 1, pltpu.roll(pair, 64, 1), pair)
                    split_out[2 + r, l : l + 1, 0:128] = first
                    split_out[2 + r, l : l + 1, 128:192] = pair[:, 0:64]
            for k in range(1, 4):
                sz_copy(k).wait_send()
                sq_copy(k).wait_send()
            sc_copy().wait_send()

        def qkv(i, l, gathered):
            def step(k, carry):
                if gathered:
                    ag_wait(i, A, l, k)
                tp = peer_t(k)
                at = rows(tp)
                here = pl.ds(pl.multiple_of(cc * tokens + tp * shard, shard), shard)
                made = dot(A[l, at], WA[l]) + BQ[l]
                q01 = made[:, 0:128].astype(BF16) * jnp.asarray(0.125, BF16)
                qk2 = made[:, 128:256]
                q2 = qk2.astype(BF16) * jnp.asarray(0.125, BF16)
                none = jnp.zeros_like(q01)
                QC[l, tp, 0:128] = jnp.where(lower, q01, none)
                QC[l, tp, 128:256] = jnp.where(lower, none, q01)
                QC[l, tp, 256:384] = jnp.where(lower, q2, none)
                v01 = made[:, 384:512]
                v2 = jnp.where(lower, 0.0, pltpu.roll(made[:, 512:640], 64, 1))
                KV[l, 0, here] = made[:, 256:384].astype(BF16)
                KV[l, 1, here] = pltpu.roll(qk2, 64, 1).astype(BF16)
                KV[l, 2, here] = v01.astype(BF16)
                KV[l, 3, here] = v2.astype(BF16)
                VT[l, cc, 0, :, at] = jnp.transpose(v01).astype(BF16)
                VT[l, cc, 1, :, at] = jnp.transpose(v2).astype(BF16)
                return carry

            lax.fori_loop(0, 4, step, 0)
            kv_copy(l).start()
            vt_copy(l, cc).start()

        def kv_copy(l):
            at = KV.at[l, :, pl.ds(pl.multiple_of(cc * tokens, tokens), tokens)]
            return remote(at, at, kv_base[l], sib)

        def vt_copy(l, c):
            return remote(VT.at[l, c], VT.at[l, c], kv_base[l] + 1, sib)

        def kv_wait(l):
            at = KV.at[l, :, pl.ds(pl.multiple_of((1 - cc) * tokens, tokens), tokens)]
            remote(at, at, kv_base[l], sib).wait_recv()
            vt_copy(l, 1 - cc).wait_recv()

        def kv_drain(l):
            kv_copy(l).wait_send()
            vt_copy(l, cc).wait_send()

        def attend(l, hook=None):
            def weigh(scores):
                highest = jnp.max(scores, axis=0, keepdims=True)
                raised = jnp.exp(scores - highest)
                return raised.astype(BF16), 1.0 / jnp.sum(raised, axis=0, keepdims=True)

            def mix(tile, low):
                return dot(VT[l, 0, tile], low[0:tokens]) + dot(VT[l, 1, tile], low[tokens:])

            def step(s, carry):
                k = back(s)
                tp = peer_t(k)
                low, scale = weigh(dot_nt(KV[l, 0], QC[l, tp, 0:256]))
                E01[l, tp] = low
                RR[l, tp, :, 0:256] = scale
                made = mix(0, low) * scale
                both = jnp.where(top_rows, made[:, 0:128], made[:, 128:256])
                CS[k, 0:shard] = jnp.transpose(both).astype(BF16)
                low, scale = weigh(dot_nt(KV[l, 1], QC[l, tp, 256:384]))
                E2[l, tp] = low
                RR[l, tp, :, 256:384] = scale
                third = jnp.transpose(mix(1, low) * scale)
                half = shard // 2
                third = jnp.where(lower, pltpu.roll(third[0:half], 64, 1), third[half:shard])
                CS[k, shard : shard + half] = third.astype(BF16)

                @pl.when(k > 0)
                def _():
                    context_copy(l, k).start()

                if hook is not None:
                    pl.when(k == 1)(hook)
                return carry

            lax.fori_loop(0, 4, step, 0)
            CX[l, t] = CS[0]

        def context_copy(l, k):
            return remote(CS.at[k], CX.at[l, t], cx_base[l] + k - 1, peer_dev(k))

        def attended(l):
            for k in range(1, 4):
                remote(CS.at[0], CX.at[l, peer_t(k)], cx_base[l] + k - 1, sib).wait_recv()
            for b in range(4):
                CF[l, :, b * 128 : b * 128 + 128] = CX[l, b, 0:shard]
            half = shard // 2
            for b in range(2):
                even = CX[l, 2 * b, shard : shard + half].astype(F32)
                odd = CX[l, 2 * b + 1, shard : shard + half].astype(F32)
                lanes = slice(512 + b * 128, 640 + b * 128)
                first = jnp.where(lower, even, pltpu.roll(odd, 64, 1))
                second = jnp.where(lower, pltpu.roll(even, 64, 1), odd)
                CF[l, 0:half, lanes] = first.astype(BF16)
                CF[l, half:shard, lanes] = second.astype(BF16)
            for k in range(1, 4):
                context_copy(l, k).wait_send()
            return dot_nt(CF[l], WO[l])

        def expand(i_ag, i_rs, l):
            def part(k):
                ag_wait(i_ag, N, l, k)
                at = rows(peer_t(k))
                f = dot(N[l, at], W1[l]) + B1[l]
                cdf = 0.5 * (1.0 + lax.erf(f * (2.0**-0.5)))
                slope = cdf + f * jnp.exp(-0.5 * f * f) * ((2.0 * math.pi) ** -0.5)
                H[l, at] = (f * cdf).astype(BF16)
                DG[l, at] = slope.astype(BF16)
                return dot_nt(H[l, at], W2[l])

            rs_loop(i_rs, forth, part)

        def shrink_back(i_ag, i_rs, l, gathered):
            def part(k):
                if gathered:
                    ag_wait(i_ag, GY, l, k)
                at = rows(peer_t(k))
                g = dot(GY[l, at], W2[l]) * DG[l, at].astype(F32)
                GF[at, :] = g.astype(BF16)
                return dot_nt(GF[at, :], W1[l])

            rs_loop(i_rs, forth, part)

        def context_grad_copy(l, k):
            return remote(CS.at[k], GC.at[l, t], gc_base[l] + k - 1, peer_dev(k))

        def context_grads(l, value):
            GO[l] = value
            made = dot(value, WO[l])
            half = shard // 2
            for b in range(4):
                CX[l, b, 0:shard] = made[:, b * 128 : b * 128 + 128].astype(BF16)
                pair = made[:, 512 + (b // 2) * 128 : 640 + (b // 2) * 128]
                first, second = pair[0:half], pair[half:shard]
                if b % 2 == 0:
                    both = jnp.where(lower, first, pltpu.roll(second, 64, 1))
                else:
                    both = jnp.where(lower, pltpu.roll(first, 64, 1), second)
                CX[l, b, shard : shard + half] = both.astype(BF16)
            for k in (3, 1, 2):
                CS[k] = CX[l, peer_t(k)]
                context_grad_copy(l, k).start()
            GC[l, t] = CX[l, t]

        def attend_back(l, hook):
            GKV[...] = jnp.zeros_like(GKV)
            for tile in range(2):
                for half in range(2):
                    keys = KV[l, tile, half * tokens : (half + 1) * tokens]
                    VT[0, half, tile] = jnp.transpose(keys.astype(F32)).astype(BF16)

            def step(k, carry):
                tp = peer_t(k)
                at = rows(tp)

                @pl.when(k > 0)
                def _():
                    remote(
                        CS.at[0], GC.at[l, tp], gc_base[l] + k - 1, sib
                    ).wait_recv()

                pl.when(k == 1)(hook)
                scale = RR[l, tp]
                r01, r2 = scale[:, 0:256], scale[:, 256:384]
                spread = jnp.where(top_rows, scale[:, 0:128], scale[:, 128:256])
                by_row = jnp.transpose(spread)
                by_row2 = jnp.transpose(jnp.where(top_rows, 0.0, r2))
                c01 = (GC[l, tp, 0:shard].astype(F32) * by_row).astype(BF16)
                third = GC[l, tp, shard : shard + shard // 2].astype(F32)
                third = jnp.concatenate([pltpu.roll(third, 64, 1), third], axis=0)
                c2 = (third * by_row2).astype(BF16)
                none = jnp.zeros_like(c01)
                c01 = jnp.concatenate(
                    [jnp.where(lower, c01, none), jnp.where(lower, none, c01)], axis=0
                )
                made = []
                for tile, low_ref, scale, grad, lanes in (
                    (0, E01, r01, c01, slice(0, 256)),
                    (1, E2, r2, c2, slice(256, 384)),
                ):
                    gp = dot_nt(KV[l, 2 + tile], grad)
                    low = low_ref[l, tp]
                    e = low.astype(F32)
                    inner = scale * jnp.sum(e * gp, axis=0, keepdims=True)
                    gs = (e * (gp - inner)).astype(BF16)
                    GKV[tile] += dot(gs, QC[l, tp, lanes])
                    GKV[2 + tile] += dot(low, grad)
                    made.append(dot(VT[0, 0, tile], gs[0:tokens]) + dot(VT[0, 1, tile], gs[tokens:]))
                both = jnp.where(top_rows, made[0][:, 0:128], made[0][:, 128:256])
                GQ[at, 0:128] = (0.125 * jnp.transpose(both)).astype(BF16)
                third = jnp.where(lower, 0.125 * jnp.transpose(made[1]), 0.0)
                GQ[at, 128:256] = third.astype(BF16)
                return carry

            lax.fori_loop(0, 4, step, 0)
            other = pl.ds(pl.multiple_of((1 - cc) * tokens, tokens), tokens)
            for tile in range(4):
                KVS[tile] = GKV[tile, other].astype(BF16)
            gkv_copy(l).start()
            for k in range(1, 4):
                context_grad_copy(l, k).wait_send()

        def gkv_copy(l):
            return remote(KVS, KVR.at[l], gkv_base[l], sib)

        def heads_back(i, l):
            gkv_copy(l).wait_recv()
            gkv_copy(l).wait_send()

            def part(k):
                at = rows(peer_t(k))
                here = pl.ds(pl.multiple_of(cc * tokens + peer_t(k) * shard, shard), shard)
                k01, k2, v01, v2 = (
                    GKV[tile, here] + KVR[l, tile, at].astype(F32) for tile in range(4)
                )
                G[at, 0:128] = GQ[at, 0:128]
                G[at, 128:256] = (
                    GQ[at, 128:256].astype(F32) + pltpu.roll(k2, 64, 1)
                ).astype(BF16)
                G[at, 256:384] = k01.astype(BF16)
                G[at, 384:512] = v01.astype(BF16)
                G[at, 512:640] = pltpu.roll(v2, 64, 1).astype(BF16)
                return dot_nt(G[at, :], WA[l])

            rs_loop(i, back, part)

        spread_start(frames, X0, 0)
        att_b_start(0)
        att_a_piece(0, 0)
        biases_start()
        mlp_a_start(0)
        for p in range(4):
            spread_pass(X0, 0, p)
        for p in range(4):
            spread_wait(frames, X0, 0, p)
        att_a_first(0)

        def first_norm(k, carry):
            at = rows(k)
            hat, inverse = norm_parts(X0[at, :].astype(F32))
            A[0, at] = (hat * row(0, 0) + row(0, 1)).astype(BF16)
            return carry

        lax.fori_loop(0, 4, first_norm, 0)
        XS[0] = X0[rows(t), :].astype(F32)
        att_a_rest(0)
        out_b_start(0)
        mlp_b_start(0)
        biases_ready()
        att_c_start(0)
        att_ready(0)
        spread_start(cot, GY.at[top], 1)
        for l in range(layers):
            qkv(4 * l + 3, l, l > 0)
            out_a_start(l)
            kv_wait(l)
            if l == 0:
                for p in range(4):
                    spread_pass(GY.at[top], 1, p)
            attend(l, (lambda: mlp_pass(0)) if l == 0 else None)
            out_c_start(l)
            if l > 0:
                mlp_pass(l)
            out_ready(l)
            between = XS[l] + attended(l) + row(l, 2)
            MS[l] = between
            hat, inverse = norm_parts(between)
            ag_start(4 * l, N, l, (hat * row(l, 3) + row(l, 4)).astype(BF16))
            mlp_c_start(l)
            mlp_ready(l)
            if l + 1 < layers:
                att_b_start(l + 1)
                out_b_start(l + 1)
            expand(4 * l, l, l)
            if l + 1 < layers:
                mlp_a_start(l + 1)
                att_a_piece(l + 1, 0)
                att_a_first(l + 1)
                att_a_rest(l + 1)
                mlp_b_start(l + 1)
                total = rs_finish(l)
                stream = MS[l] + total + row(l, 5)
                XS[l + 1] = stream
                hat, inverse = norm_parts(stream)
                normed = (hat * row(l + 1, 0) + row(l + 1, 1)).astype(BF16)
                ag_start(4 * l + 7, A, l + 1, normed)
                att_c_start(l + 1)
                att_ready(l + 1)
            else:
                total = rs_finish(l)
                out_start(0, MS[l] + total + row(l, 5))

        spread_drain(frames, X0, 0)
        for l in range(layers):
            kv_drain(l)
        for p in range(4):
            spread_wait(cot, GY.at[top], 1, p)
        GS[...] = GY[top, rows(t)].astype(F32)
        rs_next = layers
        for l in reversed(range(layers)):
            shrink_back(4 * l + 2, rs_next, l, l < top)
            mlp_grads(l)
            mlp_grad_b(l)
            mlp_sum[l][0]()
            grad = GS[...]
            SMALL[8 * l + 5 : 8 * l + 6, :] = jnp.sum(grad, axis=0, keepdims=True)
            gn = rs_finish(rs_next)
            rs_next += 1
            hat, inverse = norm_parts(MS[l])
            gm = grad + norm_back(gn, hat, inverse, row(l, 3))
            context_grads(l, gm.astype(BF16))
            GS[...] = gm
            SMALL[8 * l + 3 : 8 * l + 4, :] = jnp.sum(gn * hat, axis=0, keepdims=True)
            SMALL[8 * l + 4 : 8 * l + 5, :] = jnp.sum(gn, axis=0, keepdims=True)
            SMALL[8 * l + 2 : 8 * l + 3, :] = jnp.sum(gm, axis=0, keepdims=True)
            if l < top:
                att_grad_a(l + 1)
            out_grads(l)

            def hook(l=l):
                if l == top:
                    out_z[0][1]()
                    out_forward(0, (0, 2))
                out_grad_a(l)

            attend_back(l, hook)
            if l < top:
                att_grad_b(l + 1)
            heads_back(rs_next, l)
            mlp_sum[l][1]()
            att_grads(l)
            out_grad_b(l)
            if l < top:
                att_sum[l + 1][1]()
            if l == 0:
                att_grad_a(l)
            gn = rs_finish(rs_next)
            rs_next += 1
            hat, inverse = norm_parts(XS[l])
            gx = GS[...] + norm_back(gn, hat, inverse, row(l, 0))
            if l > 0:
                ag_start(4 * l - 2, GY, l - 1, gx.astype(BF16))
                GS[...] = gx
            SMALL[8 * l : 8 * l + 1, :] = jnp.sum(gn * hat, axis=0, keepdims=True)
            SMALL[8 * l + 1 : 8 * l + 2, :] = jnp.sum(gn, axis=0, keepdims=True)
            if l == 0:
                small_z()
                out_start(1, gx)
                out_forward(1, (0,))
            else:
                out_grad_end(l)
        small_c()
        if layers > 1:
            mlp_grad_a(1)
        att_grad_b(0)
        out_forward(0, (1, 3))
        if layers > 1:
            mlp_grad_end(1)
        mlp_grad_a(0)
        small_q()
        out_z[1][1]()
        out_forward(1, (2,))
        att_sum[0][1]()
        out_forward(1, (1, 3))
        if layers > 1:
            att_grad_end(1)
        mlp_grad_end(0)
        out_grad_end(0)
        small_end()
        out_finish(0, enc)
        att_grad_end(0)
        out_finish(1, xg)

        spread_drain(cot, GY.at[top], 1)
        for l in range(layers):
            att_drain(l)
            ag_drain(4 * l, N, l)
            out_drain(l)
            if l < top:
                ag_drain(4 * l + 2, GY, l)
            if l > 0:
                ag_drain(4 * l + 3, A, l)

    return kernel


def fused_step(frames, cot, hw, mw, wm, shared, sv):
    layers, rows_of, _ = mw.shape
    tokens, width = frames.shape
    shard = tokens // 4
    numbers = Numbers()
    kernel = make_kernel(layers, tokens, width, numbers)
    two = 2 * tokens
    v = pltpu.VMEM
    scratch = [
        v((layers, shard, width), F32),
        v((layers, shard, width), F32),
        v((layers, tokens, width), BF16),
        v((layers, tokens, width), BF16),
        v((layers, shard, width), BF16),
        v((layers, tokens, width), BF16),
        v((shard, width), F32),
        v((layers, width, 640), BF16),
        v((layers, width, width), BF16),
        v((layers, width, width), BF16),
        v((layers, width, width), BF16),
        v((layers, 4, rows_of, 640), BF16),
        v((layers, 4, rows_of, 256), BF16),
        v((layers, 2, 4, 4, rows_of, width // 2), BF16),
        v((layers, 4, 3 * shard, 128), BF16),
        v((layers, 4, two, 128), BF16),
        v((layers, 2, 2, 128, tokens), BF16),
        v((layers, 4, two, 2 * shard), BF16),
        v((layers, 4, two, shard), BF16),
        v((layers, 4, 1, 3 * shard), F32),
        v((4, 3 * shard // 2, 128), BF16),
        v((layers, 4, 3 * shard // 2, 128), BF16),
        v((layers, shard, width), BF16),
        v((layers, 4, 3 * shard // 2, 128), BF16),
        v((layers, tokens, width), BF16),
        v((layers, tokens, width), BF16),
        v((tokens, width), BF16),
        v((tokens, 256), BF16),
        v((tokens, 640), BF16),
        v((4, two, 128), F32),
        v((4, tokens, 128), BF16),
        v((layers, 4, tokens, 128), BF16),
        v((shard, width), F32),
        v((4, shard, width), BF16),
        v((2, 3, shard, width), BF16),
        v((4, 4, rows_of, width // 2), BF16),
        v((layers, 3, 4, rows_of, width // 2), BF16),
        v((4, rows_of, width // 2), BF16),
        v((layers, 4, rows_of, width // 2), BF16),
        v((layers, 4, rows_of, width // 2), BF16),
        v((layers, rows_of, 640), BF16),
        v((2, 4, rows_of, 640), BF16),
        v((4, rows_of, 640), BF16),
        v((layers, 4, rows_of, 640), BF16),
        v((layers, 3, rows_of, 640), BF16),
        v((2, 4, rows_of, width), BF16),
        v((4, rows_of, width), BF16),
        v((layers, 3, rows_of, width), BF16),
        v((4, rows_of, 256), BF16),
        v((layers, 3, rows_of, 256), BF16),
        v((2, 4, shard, width), BF16),
        v((4, layers, 8, 256), F32),
        v((layers, 1, 640), F32),
        v((layers, 1, width), F32),
        v((8 * layers, width), F32),
        v((3, 8 * layers, width), F32),
        v((8 * layers, width), F32),
        v((4, 8 * layers, width), F32),
        pltpu.SemaphoreType.DMA((numbers.count,)),
        pltpu.SemaphoreType.DMA((numbers.count,)),
        pltpu.SemaphoreType.DMA((4,)),
    ]
    inside = pl.BlockSpec(memory_space=pltpu.VMEM)
    outside = pl.BlockSpec(memory_space=pl.ANY)
    return pl.pallas_call(
        kernel,
        out_shape=(
            jax.ShapeDtypeStruct((4, shard, width), BF16),
            jax.ShapeDtypeStruct((4, shard, width), BF16),
            jax.ShapeDtypeStruct((layers, 3, rows_of, width // 4), BF16),
            jax.ShapeDtypeStruct((layers, rows_of, width // 4), BF16),
            jax.ShapeDtypeStruct((layers, 4, rows_of, width // 2), BF16),
            jax.ShapeDtypeStruct((6, layers, width), F32),
            jax.ShapeDtypeStruct((6, layers, width // 4), F32),
        ),
        in_specs=[outside, outside] + [inside] * 5,
        out_specs=(outside, outside) + (inside,) * 5,
        scratch_shapes=scratch,
        compiler_params=pltpu.CompilerParams(
            collective_id=0, has_side_effects=True, vmem_limit_bytes=63 * 1024 * 1024
        ),
    )(frames, cot, hw, mw, wm, shared, sv)


def adam_update(weight, gradient, first_moment, second, step_rate):
    first_new = beta_one * first_moment + (1.0 - beta_one) * gradient
    second_new = beta_two * second + (1.0 - beta_two) * gradient * gradient
    bias_one = 1.0 - beta_one**STEP
    bias_two = 1.0 - beta_two**STEP
    direction = first_new / bias_one / (jnp.sqrt(second_new / bias_two) + adam_epsilon)
    return (second_new, weight - step_rate * (direction + weight_decay * weight))


RATES = (0.1, 0.1, 0.1, 0.1, 2.0, 0.5)


def finish_kernel(*refs):
    enc, xg, pairs = refs[0:3]
    outs = refs[25:]
    groups, at = [], 3
    for i in range(6):
        packed = i in (2, 3)
        grad = (outs[2 + 3 * i],) if packed else (refs[at],)
        at += 0 if packed else 1
        groups.append(grad + tuple(refs[at : at + 3]))
        at += 3
    for r in range(4):
        total = pairs[0, r].astype(F32)
        third = pltpu.roll(total[:, 128:256], 64, 1)
        outs[8][0, :, r, :] = total[:, 0:192]
        outs[11][0, :, r, 0:128] = total[:, 256:384]
        outs[11][0, :, r, 128:192] = third[:, 0:64]
    outs[0][...] = enc[...].astype(F32)
    outs[1][...] = xg[...].astype(F32)
    for i, (grad, weight, first, second) in enumerate(groups):
        g = grad[...].astype(F32)
        renewed, updated = adam_update(weight[...], g, first[...], second[...], RATES[i])
        if i not in (2, 3):
            outs[2 + 3 * i][...] = g
        outs[3 + 3 * i][...] = renewed
        outs[4 + 3 * i][...] = updated


def finish(enc, xg, pairs, groups):
    layers, _, rows_of, wide = groups[0][0].shape
    tokens, width = enc.shape
    cut = 2 if rows_of % 16 == 0 else 1
    steps = layers * cut
    part = rows_of // cut
    stream = pl.BlockSpec((tokens // steps, width), lambda l, h: (cut * l + h, 0))
    heads = pl.BlockSpec((1, 3, part, wide), lambda l, h: (l, 0, h, 0))
    flat = pl.BlockSpec((1, part, wide), lambda l, h: (l, h, 0))
    grid = pl.BlockSpec((1, part, 4, wide), lambda l, h: (l, h, 0, 0))
    shared = pl.BlockSpec((6, layers, width), lambda l, h: (0, 0, 0))
    split = pl.BlockSpec((6, layers, wide), lambda l, h: (0, 0, 0))
    kinds = (heads, flat, grid, grid, shared, split)
    both = pl.BlockSpec((1, 4, part, 2 * wide), lambda l, h: (l, 0, h, 0))
    shapes = [jax.ShapeDtypeStruct((tokens, width), F32)] * 2
    out_specs = [stream, stream]
    for kind, group in zip(kinds, groups):
        shapes += [jax.ShapeDtypeStruct(group[-1].shape, F32)] * 3
        out_specs += [kind] * 3
    return pl.pallas_call(
        finish_kernel,
        grid=(layers, cut),
        out_shape=shapes,
        in_specs=[stream, stream, both]
        + [kind for kind, group in zip(kinds, groups) for _ in group],
        out_specs=out_specs,
        compiler_params=pltpu.CompilerParams(
            dimension_semantics=("arbitrary", "arbitrary"),
            vmem_limit_bytes=63 * 1024 * 1024,
        ),
    )(enc, xg, pairs, *[v for group in groups for v in group])


def shards(
    frames, cotangent, heads_weight, merge_weight, expand_weight, shrink_weight,
    shared_vectors, split_vectors,
    heads_first, heads_second, merge_first, merge_second, expand_first, expand_second,
    shrink_first, shrink_second, shared_first, shared_second, split_first, split_second,
):
    groups = lax.axis_size("dp") // 4
    width = frames.shape[-1]
    dp_group = [[lo + 4 * h for h in range(groups)] for lo in range(4)]

    def to_kernel(v):
        if groups == 1:
            return v
        part = v.reshape(v.shape[:-1] + (groups, 8, width // (8 * groups)))
        return jnp.swapaxes(part, -3, -2).reshape(v.shape)

    def from_kernel(v):
        if groups == 1:
            return v
        part = v.reshape(v.shape[:-1] + (8, groups, width // (8 * groups)))
        return jnp.swapaxes(part, -3, -2).reshape(v.shape)

    def widen(v, axis):
        if groups == 1:
            return v
        return lax.all_gather(
            v, "dp", axis=axis, tiled=True, axis_index_groups=dp_group
        )

    def narrow(v, axis):
        if groups == 1:
            return v
        return lax.psum_scatter(
            v.astype(BF16),
            "dp",
            scatter_dimension=axis,
            tiled=True,
            axis_index_groups=dp_group,
        ).astype(F32)

    e = jnp.swapaxes(expand_weight.astype(BF16), 1, 2)
    s = jnp.swapaxes(shrink_weight.astype(BF16), 1, 2)
    wm = jnp.concatenate([e, s[..., 128:], s[..., :128]], axis=-1)
    wm = widen(wm, 2)
    hw, mw = jnp.swapaxes(heads_weight, 1, 2), merge_weight
    if groups > 1:
        hw = widen(hw.astype(BF16), 2).astype(F32)
        mw = widen(mw.astype(BF16), 1).astype(F32)

    enc, xg, heads_grad, merge_grad, pairs, shared_grad, split_grad = (
        fused_step(
            to_kernel(frames[0]),
            to_kernel(cotangent[0]),
            hw,
            mw,
            wm,
            jnp.swapaxes(to_kernel(shared_vectors), 0, 1),
            jnp.swapaxes(split_vectors, 0, 1),
        )
    )
    enc, xg = (from_kernel(v.reshape(frames.shape[1:])) for v in (enc, xg))
    heads_grad = narrow(heads_grad, 2)
    merge_grad = narrow(merge_grad, 1)
    pairs = narrow(pairs, 2)
    shared_grad = from_kernel(shared_grad)
    if groups > 1:
        shared_grad = lax.psum(shared_grad, "dp", axis_index_groups=dp_group)
        split_grad = lax.psum(split_grad, "dp", axis_index_groups=dp_group)

    def turned(v):
        return jnp.swapaxes(v, 1, 2)

    def lined(v):
        return jnp.swapaxes(v, 0, 1)

    def same(v):
        return v

    table = (
        (turned, (heads_grad,), heads_weight, heads_first, heads_second),
        (same, (merge_grad,), merge_weight, merge_first, merge_second),
        (same, (), expand_weight, expand_first, expand_second),
        (same, (), shrink_weight, shrink_first, shrink_second),
        (lined, (shared_grad,), shared_vectors, shared_first, shared_second),
        (lined, (split_grad,), split_vectors, split_first, split_second),
    )
    groups_in = [g + tuple(view(v) for v in rest) for view, g, *rest in table]
    done = finish(enc, xg, pairs, groups_in)
    out = [done[0][None], done[1][None]]
    for i, (view, *_) in enumerate(table):
        out += [view(v) for v in done[2 + 3 * i : 5 + 3 * i]]
    return tuple(out)


def solution(mesh):
    rows = ("dp", "seq")
    stream = P("dp", "seq", None)
    wide = P(None, rows, None, "tensor")
    flat = P(None, rows, "tensor")
    split = P(None, None, "tensor")
    return jax.shard_map(
        shards,
        mesh=mesh,
        in_specs=(
            stream, stream, wide, flat, wide, wide, P(), split,
            wide, wide, flat, flat, wide, wide, wide, wide, P(), P(), split, split,
        ),
        out_specs=(stream, stream)
        + (wide,) * 3 + (flat,) * 3 + (wide,) * 6 + (P(),) * 3 + (split,) * 3,
        check_vma=False,
    )
```

```python
import math

import jax
import jax.numpy as jnp
from jax import lax
from jax.experimental import pallas as pl
from jax.experimental.pallas import tpu as pltpu
from jax.sharding import PartitionSpec as P

HEAD_DIM = 64
STEP = 10

beta_one = 0.9
beta_two = 0.999
adam_epsilon = 1e-08
weight_decay = 0.01
norm_epsilon = 1e-05

MESH = pl.DeviceIdType.MESH
F32 = jnp.float32
BF16 = jnp.bfloat16


def dot(a, b):
    return lax.dot_general(a, b, (((1,), (0,)), ((), ())), preferred_element_type=F32)


def dot_nt(a, b):
    return lax.dot_general(a, b, (((1,), (1,)), ((), ())), preferred_element_type=F32)


def dot_tn(a, b):
    return lax.dot_general(a, b, (((0,), (0,)), ((), ())), preferred_element_type=F32)


def norm_parts(values):
    centre = values - jnp.mean(values, axis=-1, keepdims=True)
    spread = jnp.mean(centre * centre, axis=-1, keepdims=True)
    inverse = lax.rsqrt(spread + norm_epsilon)
    return centre * inverse, inverse


def norm_back(grad, hat, inverse, gain):
    scaled = grad * gain
    first = jnp.mean(scaled, axis=-1, keepdims=True)
    second = jnp.mean(scaled * hat, axis=-1, keepdims=True)
    return inverse * (scaled - first - hat * second)


class Numbers:
    def __init__(self):
        self.count = 0

    def take(self, n):
        base = self.count
        self.count += n
        return base


def make_kernel(layers, tokens, width, numbers):
    shard = tokens // 4
    rows_of = 96
    take = numbers.take
    rs_base = [take(3) for _ in range(3 * layers)]
    ag_base = [take(4) for _ in range(4 * layers)]
    sp_base = [take(16), take(16)]
    sv_base, sz_base, sc_base, sq_base = take(3), take(3), take(1), take(3)
    cx_base = [take(3) for _ in range(layers)]
    gc_base = [take(3) for _ in range(layers)]
    ob, oa, oc = ([take(n) for _ in range(layers)] for n in (3, 3, 4))
    goc, goa, gob = ([take(n) for _ in range(layers)] for n in (1, 3, 3))
    kv_base = [take(2) for _ in range(layers)]
    gkv_base = [take(1) for _ in range(layers)]
    ab, aa, ac = ([take(n) for _ in range(layers)] for n in (4, 3, 4))
    ma, mb, mc = ([take(n) for _ in range(layers)] for n in (3, 4, 4))
    gac, gaa, gab = ([take(n) for _ in range(layers)] for n in (1, 3, 4))
    gmc, gmb, gma = ([take(n) for _ in range(layers)] for n in (1, 4, 3))
    oz = [take(4) for _ in range(2)]
    op = [take(4) for _ in range(2)]
    top = layers - 1

    def kernel(
        frames, cot, hw, mw, wm, shared, sv,
        enc, xg, gh_out, go_out, gm_out, shared_out, split_out,
        XS, MS, A, N, GO, GY, GS,
        WA, WO, W1, W2, T, GA, GB, GM,
        QC, KV, VT, E01, E2, RR, CS, CX, CF, GC, H, DG, GF, GQ, G,
        GKV, KVS, KVR,
        OWN, RSS, RSR,
        CM, BM, TM, UM,
        FM, FA, SA, CA, RA, RB, SO, CO, RO, TO, RP,
        EZ, SV, BQ, B1, SMALL, SZ, SC, SP,
        ssem, rsem, lsem,
    ):
        dp = lax.axis_index("dp")
        y = lax.axis_index("seq")
        z = lax.axis_index("tensor")
        hi = lax.div(dp, 4)
        lo = lax.rem(dp, 4)
        xx = lax.div(lo, 2)
        cc = lax.rem(lo, 2)
        t = 2 * xx + y

        def flip(bit, by):
            return bit + by - 2 * bit * by

        def peer(k):
            if isinstance(k, int):
                kx, ky = k // 2, k % 2
            else:
                kx, ky = lax.div(k, 2), lax.rem(k, 2)
            return flip(xx, kx), flip(y, ky)

        def peer_t(k):
            px, py = peer(k)
            return 2 * px + py

        def peer_dev(k):
            px, py = peer(k)
            return {"dp": 4 * hi + 2 * px + cc, "seq": py}

        def peer_j(k):
            px, py = peer(k)
            return 4 * px + 2 * cc + py

        my_j = 4 * xx + 2 * cc + y
        sib = {"dp": dp + 1 - 2 * cc}

        def z_to(k):
            return lax.rem(z + k, 4)

        def z_from(k):
            return lax.rem(z + 4 - k, 4)

        middle = jnp.logical_or(z == 1, z == 2)

        def z_near(k, act):
            if k == 2:
                act()
            else:
                pl.when(z != (3 if k == 1 else 0))(act)

        def z_far(k, act):
            pl.when(z == (3 if k == 1 else 0))(act)

        def z_come(k, act):
            pl.when(z != (0 if k == 1 else 3))(act)

        def gather_z(slot, base):
            def copy(k):
                return remote(slot(z), slot(z), base + k - 1, {"tensor": z_to(k)})

            def relay():
                far = slot(z_from(2))
                return remote(
                    far, far, base + 2 * (z - 1), {"tensor": 3 * (z - 1)}, send=base + 3
                )

            def wait(k):
                remote(slot(z), slot(z_from(k)), base + k - 1, sib).wait_recv()

            def start():
                for k in (2, 1, 3):
                    z_near(k, lambda k=k: copy(k).start())

            def pass_on():
                wait(2)
                pl.when(middle)(lambda: relay().start())

            def drain():
                for k in (2, 1, 3):
                    z_near(k, lambda k=k: copy(k).wait_send())
                pl.when(middle)(lambda: relay().wait_send())

            return start, pass_on, wait, drain

        def sum_z(part, far, landing, base):
            def copy(k):
                return remote(part(z_to(k)), landing(k), base + k - 1, {"tensor": z_to(k)})

            def far_copy():
                end = lax.div(z, 3)
                return remote(part(3 - z), far, base + 3, {"tensor": 1 + end})

            def start_far():
                pl.when(jnp.logical_not(middle))(lambda: far_copy().start())

            def start():
                for k in (1, 3):
                    z_near(k, lambda k=k: copy(k).start())
                    at = landing(k)

                    @pl.when(z == (0 if k == 1 else 3))
                    def _(at=at):
                        at[...] = jnp.zeros(at.shape, BF16)

                pl.when(jnp.logical_not(middle))(lambda: copy(2).start())

            def combine():
                @pl.when(middle)
                def _():
                    far_copy().wait_recv()
                    at = part(z_to(2))
                    at[...] = (at[...].astype(F32) + far[...].astype(F32)).astype(BF16)
                    copy(2).start()

            def wait():
                copy(2).wait_recv()
                for k in (1, 3):
                    z_come(k, lambda k=k: copy(k).wait_recv())

            def drain():
                copy(2).wait_send()
                for k in (1, 3):
                    z_near(k, lambda k=k: copy(k).wait_send())
                pl.when(jnp.logical_not(middle))(lambda: far_copy().wait_send())

            return start, combine, wait, drain, start_far

        def remote(src, dst, number, dev, send=None):
            send = number if send is None else send
            return pltpu.make_async_remote_copy(
                src_ref=src,
                dst_ref=dst,
                send_sem=ssem.at[send],
                recv_sem=rsem.at[number],
                device_id=dev,
                device_id_type=MESH,
            )

        def rows(k_t):
            return pl.ds(pl.multiple_of(k_t * shard, shard), shard)

        def block(j):
            return pl.ds(pl.multiple_of(j * rows_of, rows_of), rows_of)

        X0 = GF
        lower = lax.broadcasted_iota(jnp.int32, (1, 128), 1) < 64
        top_rows = lax.broadcasted_iota(jnp.int32, (128, 1), 0) < 64

        barrier = pltpu.get_barrier_semaphore()
        for k in range(1, 8):
            dev = {
                "dp": 4 * hi + 2 * flip(xx, k // 4) + flip(cc, (k // 2) % 2),
                "seq": flip(y, k % 2),
            }
            pl.semaphore_signal(barrier, inc=1, device_id=dev, device_id_type=MESH)
        for k in range(1, 4):
            pl.semaphore_signal(
                barrier, inc=1, device_id={"tensor": z_to(k)}, device_id_type=MESH
            )
        pl.semaphore_wait(barrier, 10)

        xs = lax.div(z, 2)
        source = jnp.logical_and(lo == z, y == cc)
        relay = jnp.logical_and(xx != xs, y == cc)
        relay_dev = {"dp": dp, "seq": 1 - y}

        def piece(p):
            return pl.ds(p * shard, shard)

        def spread_each(src, dst, i, act, act_own):
            @pl.when(lo == z)
            def _():
                for p in range(4):
                    for d, (dx, dy) in enumerate(((1, 0), (0, 1), (0, 0))):
                        same = jnp.logical_and(cc == y, (dx, dy) == (0, 0))
                        dev = {"dp": 4 * hi + 2 * flip(xx, dx) + y, "seq": flip(y, dy)}

                        @pl.when(jnp.logical_not(same))
                        def _(p=p, d=d, dev=dev):
                            act(
                                remote(
                                    src.at[piece(p)],
                                    dst.at[piece(p)],
                                    sp_base[i] + p,
                                    dev,
                                    send=sp_base[i] + 4 + 3 * p + d,
                                )
                            )

            if act_own is not None:

                @pl.when(source)
                def _():
                    act_own(pltpu.make_async_copy(src, dst, lsem.at[i]))

        def spread_start(src, dst, i):
            spread_each(src, dst, i, lambda c: c.start(), lambda c: c.start())

        def relay_copy(dst, i, p):
            return remote(
                dst.at[piece(p)],
                dst.at[piece(p)],
                sp_base[i] + p,
                relay_dev,
                send=sp_base[i] + 4 + p,
            )

        def spread_pass(dst, i, p):
            @pl.when(relay)
            def _():
                relay_copy(dst, i, p).wait_recv()
                relay_copy(dst, i, p).start()

        def spread_wait(src, dst, i, p):
            if p == 0:

                @pl.when(source)
                def _():
                    pltpu.make_async_copy(src, dst, lsem.at[i]).wait()

            @pl.when(jnp.logical_not(jnp.logical_or(source, relay)))
            def _():
                relay_copy(dst, i, p).wait_recv()

        def spread_drain(src, dst, i):
            spread_each(src, dst, i, lambda c: c.wait_send(), None)

            @pl.when(relay)
            def _():
                for p in range(4):
                    relay_copy(dst, i, p).wait_send()

        att_z = [gather_z(lambda b, l=l: GA.at[l, b], ab[l]) for l in range(layers)]
        mlp_z = [gather_z(lambda b, l=l: GM.at[l, cc, b], mb[l]) for l in range(layers)]
        out_z = [gather_z(lambda b, i=i: EZ.at[i, b], oz[i]) for i in range(2)]

        def att_b_start(l):
            q, k, v = (hw[l, i].astype(BF16) for i in range(3))
            GA[l, z, :, 0:128] = q[:, 0:128]
            GA[l, z, :, 128:256] = jnp.concatenate([q[:, 128:192], k[:, 128:192]], axis=1)
            GA[l, z, :, 256:384] = k[:, 0:128]
            GA[l, z, :, 384:512] = v[:, 0:128]
            third = v[:, 128:192]
            GA[l, z, :, 512:640] = jnp.concatenate([third, jnp.zeros_like(third)], axis=1)
            att_z[l][0]()

        def att_a_copy(l, b):
            bx, by = lax.div(b, 2), lax.rem(b, 2)
            k = 2 * flip(xx, bx) + flip(y, by)
            return remote(
                GA.at[l, b],
                WA.at[l, block(my_j)],
                aa[l] + k - 1,
                {"dp": 4 * hi + 2 * bx + cc, "seq": by},
            )

        def att_a_piece(l, zk):
            b = z_from(zk)

            @pl.when(b != t)
            def _():
                att_a_copy(l, b).start()

            @pl.when(b == t)
            def _():
                WA[l, block(my_j)] = GA[l, t]

        def att_a_first(l):
            att_z[l][1]()
            att_a_piece(l, 2)

        def att_a_rest(l):
            for k in (1, 3):
                att_z[l][2](k)
                att_a_piece(l, k)

        def att_c_copy(l, k):
            at = WA.at[l, block(peer_j(k))]
            return remote(at, at, ac[l] + k, sib)

        def att_c_start(l):
            att_c_copy(l, 0).start()
            for k in range(1, 4):
                remote(
                    GA.at[l, 0], WA.at[l, block(peer_j(k))], aa[l] + k - 1, sib
                ).wait_recv()
                att_c_copy(l, k).start()

        def att_ready(l):
            for k in range(4):
                px, py = peer(k)
                at = WA.at[l, block(4 * px + 2 * (1 - cc) + py)]
                remote(at, at, ac[l] + k, sib).wait_recv()

        def att_drain(l):
            att_z[l][3]()
            for k in range(1, 4):
                att_a_copy(l, peer_t(k)).wait_send()
            for k in range(4):
                att_c_copy(l, k).wait_send()

        def out_b_copy(l, k):
            return remote(GB.at[l, z], GB.at[l, z], ob[l] + k - 1, {"tensor": z_to(k)})

        def out_b_start(l):
            own = mw[l].astype(BF16)
            third = own[:, 128:192]
            none = jnp.zeros_like(third)
            odd = lax.rem(z, 2) == 1
            GB[l, z, :, 0:128] = own[:, 0:128]
            GB[l, z, :, 128:256] = jnp.where(
                odd,
                jnp.concatenate([none, third], axis=1),
                jnp.concatenate([third, none], axis=1),
            )
            for k in range(1, 4):
                out_b_copy(l, k).start()

        def out_a_copy(l, k):
            at = WO.at[l, block(my_j)]
            return remote(at, at, oa[l] + k - 1, peer_dev(k))

        def out_a_start(l):
            for k in range(1, 4):
                remote(GB.at[l, z], GB.at[l, z_from(k)], ob[l] + k - 1, sib).wait_recv()
            at = block(my_j)
            for b in range(4):
                WO[l, at, b * 128 : b * 128 + 128] = GB[l, b, :, 0:128]
            for b in range(2):
                pair = GB[l, 2 * b, :, 128:256] + GB[l, 2 * b + 1, :, 128:256]
                WO[l, at, 512 + b * 128 : 640 + b * 128] = pair
            for k in range(1, 4):
                out_a_copy(l, k).start()

        def out_c_copy(l, k):
            at = WO.at[l, block(peer_j(k))]
            return remote(at, at, oc[l] + k, sib)

        def out_c_start(l):
            out_c_copy(l, 0).start()
            for k in range(1, 4):
                at = WO.at[l, block(peer_j(k))]
                remote(at, at, oa[l] + k - 1, sib).wait_recv()
                out_c_copy(l, k).start()

        def out_ready(l):
            for k in range(4):
                px, py = peer(k)
                at = WO.at[l, block(4 * px + 2 * (1 - cc) + py)]
                remote(at, at, oc[l] + k, sib).wait_recv()

        def out_drain(l):
            for k in range(1, 4):
                out_b_copy(l, k).wait_send()
                out_a_copy(l, k).wait_send()
            for k in range(4):
                out_c_copy(l, k).wait_send()

        def mlp_a_copy(l, k):
            return remote(
                wm.at[l, peer_t(k)], GM.at[l, cc, z, t], ma[l] + k - 1, peer_dev(k)
            )

        def mlp_a_start(l):
            for k in range(1, 4):
                mlp_a_copy(l, k).start()
            GM[l, cc, z, t] = wm[l, t]

        def mlp_b_start(l):
            for k in range(1, 4):
                remote(
                    wm.at[l, 0], GM.at[l, cc, z, peer_t(k)], ma[l] + k - 1, sib
                ).wait_recv()
            mlp_z[l][0]()

        def mlp_pass(l):
            mlp_z[l][1]()

        def mlp_c_copy(l, k):
            at = GM.at[l, cc, z_from(k)]
            return remote(at, at, mc[l] + k, sib)

        def mlp_c_start(l):
            mlp_c_copy(l, 0).start()
            mlp_c_copy(l, 2).start()
            for k in (1, 3):
                mlp_z[l][2](k)
                mlp_c_copy(l, k).start()

        def mlp_ready(l):
            for k in range(4):
                at = GM.at[l, 1 - cc, z_from(k)]
                remote(at, at, mc[l] + k, sib).wait_recv()
            for k in range(4):
                mlp_c_copy(l, k).wait_send()
            for k in range(1, 4):
                mlp_a_copy(l, k).wait_send()
            mlp_z[l][3]()

            def unpack(j, carry):
                jc = lax.rem(lax.div(j, 2), 2)
                jq = 2 * lax.div(j, 4) + lax.rem(j, 2)
                at = block(j)
                mixed = []
                for b in range(4):
                    chunk = GM[l, jc, b, jq]
                    W1[l, at, b * 128 : b * 128 + 128] = chunk[:, 0:128]
                    W2[l, at, b * 128 : b * 128 + 128] = chunk[:, 256:384]
                    mixed.append(chunk[:, 128:256].astype(F32))
                for b in range(2):
                    even, odd = mixed[2 * b], mixed[2 * b + 1]
                    lanes = slice(512 + b * 128, 640 + b * 128)
                    W1[l, at, lanes] = jnp.where(
                        lower, even, pltpu.roll(odd, 64, 1)
                    ).astype(BF16)
                    W2[l, at, lanes] = jnp.where(
                        lower, pltpu.roll(even, 64, 1), odd
                    ).astype(BF16)
                return carry

            lax.fori_loop(0, 8, unpack, 0)

        def rs_copy(i, k):
            return remote(RSS.at[k], RSR.at[i % 2, k - 1], rs_base[i] + k - 1, peer_dev(k))

        def rs_loop(i, order, part):
            def step(s, carry):
                k = order(s)
                partial = part(k)
                RSS[k] = partial.astype(BF16)

                @pl.when(k == 0)
                def _():
                    OWN[...] = partial

                @pl.when(k > 0)
                def _():
                    rs_copy(i, k).start()

                return carry

            lax.fori_loop(0, 4, step, 0)

        def rs_finish(i):
            for k in range(1, 4):
                rs_copy(i, k).wait_recv()
            total = OWN[...]
            for k in range(1, 4):
                total = total + RSR[i % 2, k - 1].astype(F32)
            for k in range(1, 4):
                rs_copy(i, k).wait_send()
            return total

        def ag_copy(i, buf, l, k):
            at = buf.at[l, rows(t)]
            return remote(at, at, ag_base[i] + k - 1, peer_dev(k))

        def ag_half(buf, l, k, upper):
            start = peer_t(k) * shard + upper * (shard // 2)
            return buf.at[l, pl.ds(pl.multiple_of(start, shard // 2), shard // 2)]

        def ag_relay(i, buf, l, k):
            at = ag_half(buf, l, k, k - 1)
            return remote(at, at, ag_base[i] + k + 1, peer_dev(3 - k))

        def ag_start(i, buf, l, value):
            buf[l, rows(t)] = value
            for k in (1, 2):
                ag_copy(i, buf, l, k).start()

        def ag_wait(i, buf, l, k):
            @pl.when(k == 1)
            def _():
                for near in (1, 2):
                    at = buf.at[l, rows(peer_t(near))]
                    remote(at, at, ag_base[i] + near - 1, sib).wait_recv()
                    ag_relay(i, buf, l, near).start()

            @pl.when(k == 3)
            def _():
                for upper in (0, 1):
                    at = ag_half(buf, l, 3, upper)
                    remote(at, at, ag_base[i] + 2 + upper, sib).wait_recv()

        def ag_drain(i, buf, l):
            for k in (1, 2):
                ag_copy(i, buf, l, k).wait_send()
                ag_relay(i, buf, l, k).wait_send()

        def forth(s):
            return s

        def back(s):
            return 3 - s

        def row(l, r):
            return shared[r, l : l + 1, :]

        def out_start(i, value):
            EZ[i, z] = value.astype(BF16)
            out_z[i][0]()

        def out_p_each(i, ks, act_far, act_near):
            for k in ks:
                zs = z_from(k)
                near = jnp.logical_and(lo == zs, y == cc)

                @pl.when(near)
                def _(zs=zs):
                    act_near(
                        pltpu.make_async_copy(
                            EZ.at[i, zs], (enc, xg)[i].at[t], lsem.at[2 + i]
                        )
                    )

                @pl.when(jnp.logical_not(near))
                def _(zs=zs, k=k):
                    act_far(
                        remote(
                            EZ.at[i, zs],
                            (enc, xg)[i].at[t],
                            op[i] + t,
                            {"dp": 4 * hi + zs, "seq": cc},
                            send=op[i] + k,
                        )
                    )

        def out_forward(i, ks):
            for k in ks:
                if k % 2 == 1:
                    out_z[i][2](k)
                out_p_each(i, (k,), lambda c: c.start(), lambda c: c.start())

        def out_finish(i, out):
            for d in range(4):
                mine = jnp.logical_and(t == d, cc == y)

                @pl.when(jnp.logical_not(mine))
                def _(d=d):
                    remote(EZ.at[i, 0], out.at[d], op[i] + d, sib).wait_recv()

            out_p_each(i, range(4), lambda c: c.wait_send(), lambda c: c.wait())
            out_z[i][3]()

        def att_grad_c_copy(l):
            return remote(SA.at[1 - cc], CA, gac[l], sib)

        def att_grad_a_copy(l, k):
            return remote(
                SA.at[cc, peer_t(k)], RA.at[l, t], gaa[l] + k - 1, peer_dev(k)
            )

        att_sum = [
            sum_z(lambda b, l=l: RA.at[l, b], FA.at[l], lambda k, l=l: RB.at[l, k - 1], gab[l])
            for l in range(layers)
        ]
        mlp_sum = [
            sum_z(lambda b, l=l: GM.at[l, cc, b], FM.at[l], lambda k, l=l: BM.at[l, k - 1], gmb[l])
            for l in range(layers)
        ]

        def att_grad_a(l):
            att_grad_c_copy(l).wait_recv()

            def add(q, carry):
                SA[cc, q] = (
                    SA[cc, q].astype(F32) + CA[q].astype(F32)
                ).astype(BF16)
                return carry

            lax.fori_loop(0, 4, add, 0)
            for k in range(1, 4):
                att_grad_a_copy(l, k).start()
            RA[l, t] = SA[cc, t]
            att_grad_c_copy(l).wait_send()

        def att_grad_b(l):
            for k in range(1, 4):
                remote(
                    SA.at[0, 0], RA.at[l, peer_t(k)], gaa[l] + k - 1, sib
                ).wait_recv()
            att_sum[l][4]()
            att_sum[l][0]()
            for k in range(1, 4):
                att_grad_a_copy(l, k).wait_send()

        def att_grad_end(l):
            total = RA[l, z].astype(F32)
            att_sum[l][2]()
            for k in range(1, 4):
                total = total + RB[l, k - 1].astype(F32)
            gh_out[l, 0, :, :] = total[:, 0:192].astype(BF16)
            gh_out[l, 1, :, 0:128] = total[:, 256:384].astype(BF16)
            k2 = pltpu.roll(total[:, 128:256], 64, 1)[:, 0:64]
            gh_out[l, 1, :, 128:192] = k2.astype(BF16)
            gh_out[l, 2, :, :] = total[:, 384:576].astype(BF16)
            att_sum[l][3]()

        def out_grad_c_copy(l):
            return remote(SO.at[1 - cc], CO, goc[l], sib)

        def out_grad_a_copy(l, k):
            return remote(SO.at[cc, peer_t(k)], RO.at[l, k - 1], goa[l] + k - 1, peer_dev(k))

        def out_grad_b_copy(l, k):
            return remote(
                TO.at[z_to(k)], RP.at[l, k - 1], gob[l] + k - 1, {"tensor": z_to(k)}
            )

        def out_grads(l):
            def product(b, carry):
                lanes = pl.ds(pl.multiple_of(b * 128, 128), 128)
                W2[l, lanes, :] = dot_tn(GO[l, :, lanes], CF[l]).astype(BF16)
                return carry

            lax.fori_loop(0, 6, product, 0)

            def pack(j, carry):
                jc = lax.rem(lax.div(j, 2), 2)
                jq = 2 * lax.div(j, 4) + lax.rem(j, 2)
                SO[jc, jq] = W2[l, block(j), :]
                return carry

            lax.fori_loop(0, 8, pack, 0)
            out_grad_c_copy(l).start()

        def out_grad_a(l):
            out_grad_c_copy(l).wait_recv()

            def add(q, carry):
                SO[cc, q] = (SO[cc, q].astype(F32) + CO[q].astype(F32)).astype(BF16)
                return carry

            lax.fori_loop(0, 4, add, 0)
            for k in range(1, 4):
                out_grad_a_copy(l, k).start()
            out_grad_c_copy(l).wait_send()

        def out_grad_b(l):
            total = SO[cc, t].astype(F32)
            for k in range(1, 4):
                out_grad_a_copy(l, k).wait_recv()
                total = total + RO[l, k - 1].astype(F32)
            total = total.astype(BF16)
            for b in range(4):
                TO[b, :, 0:128] = total[:, b * 128 : b * 128 + 128]
                pair = 512 + (b // 2) * 128
                TO[b, :, 128:256] = total[:, pair : pair + 128]
            for k in range(1, 4):
                out_grad_b_copy(l, k).start()
            for k in range(1, 4):
                out_grad_a_copy(l, k).wait_send()

        def out_grad_end(l):
            total = TO[z].astype(F32)
            for k in range(1, 4):
                out_grad_b_copy(l, k).wait_recv()
                total = total + RP[l, k - 1].astype(F32)
            go_out[l, :, 0:128] = total[:, 0:128].astype(BF16)
            pair = total[:, 128:256]
            pair = jnp.where(lax.rem(z, 2) == 1, pltpu.roll(pair, 64, 1), pair)
            go_out[l, :, 128:192] = pair[:, 0:64].astype(BF16)
            for k in range(1, 4):
                out_grad_b_copy(l, k).wait_send()

        def mlp_grad_c_copy(l):
            return remote(GM.at[l, 1 - cc], CM, gmc[l], sib)

        def mlp_grad_a_copy(l, k):
            return remote(TM.at[peer_t(k)], UM.at[l, t], gma[l] + k - 1, peer_dev(k))

        def mlp_grad_b(l):
            mlp_grad_c_copy(l).wait_recv()

            def add(s, carry):
                zs, q = lax.div(s, 4), lax.rem(s, 4)
                GM[l, cc, zs, q] = (
                    GM[l, cc, zs, q].astype(F32) + CM[zs, q].astype(F32)
                ).astype(BF16)
                return carry

            lax.fori_loop(0, 16, add, 0)
            mlp_sum[l][4]()
            mlp_grad_c_copy(l).wait_send()

        def mlp_grad_a(l):
            mlp_sum[l][2]()
            for q in range(4):
                total = GM[l, cc, z, q].astype(F32)
                for k in range(1, 4):
                    total = total + BM[l, k - 1, q].astype(F32)
                TM[q] = total.astype(BF16)
            for k in range(1, 4):
                mlp_grad_a_copy(l, k).start()
            UM[l, t] = TM[t]

        def mlp_grad_end(l):
            for k in range(1, 4):
                remote(TM.at[0], UM.at[l, peer_t(k)], gma[l] + k - 1, sib).wait_recv()
            gm_out[l] = UM[l]
            for k in range(1, 4):
                mlp_grad_a_copy(l, k).wait_send()
            mlp_sum[l][3]()

        def mlp_grads(l):
            def product(b, carry):
                lanes = pl.ds(pl.multiple_of(b * 128, 128), 128)
                W2[l, lanes, :] = dot_tn(GY[l, :, lanes], H[l]).astype(BF16)
                W1[l, lanes, :] = dot_tn(N[l, :, lanes], GF[...]).astype(BF16)
                return carry

            lax.fori_loop(0, 6, product, 0)

            def pack(j, carry):
                jc = lax.rem(lax.div(j, 2), 2)
                jq = 2 * lax.div(j, 4) + lax.rem(j, 2)
                at = block(j)
                for b in range(4):
                    lanes = slice(b * 128, b * 128 + 128)
                    GM[l, jc, b, jq, :, 0:128] = W1[l, at, lanes]
                    GM[l, jc, b, jq, :, 256:384] = W2[l, at, lanes]
                for b in range(2):
                    lanes = slice(512 + b * 128, 640 + b * 128)
                    one, two = W1[l, at, lanes].astype(F32), W2[l, at, lanes].astype(F32)
                    GM[l, jc, 2 * b, jq, :, 128:256] = jnp.where(
                        lower, one, pltpu.roll(two, 64, 1)
                    ).astype(BF16)
                    GM[l, jc, 2 * b + 1, jq, :, 128:256] = jnp.where(
                        lower, pltpu.roll(one, 64, 1), two
                    ).astype(BF16)
                return carry

            lax.fori_loop(0, 8, pack, 0)
            mlp_grad_c_copy(l).start()
            SMALL[8 * l + 7 : 8 * l + 8, :] = jnp.sum(GF[...].astype(F32), axis=0, keepdims=True)

        def att_grads(l):
            def product(b, carry):
                lanes = pl.ds(pl.multiple_of(b * 128, 128), 128)
                W1[l, lanes, 0:640] = dot_tn(A[l, :, lanes], G[...]).astype(BF16)
                return carry

            lax.fori_loop(0, 6, product, 0)

            def pack(j, carry):
                jc = lax.rem(lax.div(j, 2), 2)
                jq = 2 * lax.div(j, 4) + lax.rem(j, 2)
                SA[jc, jq] = W1[l, block(j), 0:640]
                return carry

            lax.fori_loop(0, 8, pack, 0)
            att_grad_c_copy(l).start()
            SMALL[8 * l + 6 : 8 * l + 7, 0:640] = jnp.sum(G[...].astype(F32), axis=0, keepdims=True)
            SMALL[8 * l + 6 : 8 * l + 7, 640:768] = jnp.zeros((1, 128), F32)

        def sv_copy(k):
            return remote(SV.at[z], SV.at[z], sv_base + k - 1, {"tensor": z_to(k)})

        def biases_start():
            SV[z] = jnp.zeros((layers, 8, 256), F32)
            for l in range(layers):
                for r in range(6):
                    SV[z, l, r : r + 1, 0:192] = sv[r, l : l + 1, :]
            for k in range(1, 4):
                sv_copy(k).start()

        def biases_ready():
            for k in range(1, 4):
                remote(SV.at[z], SV.at[z_from(k)], sv_base + k - 1, sib).wait_recv()
            for l in range(layers):
                BQ[l, :, 0:256] = SV[t, l, 0:1, :]
                BQ[l, :, 256:384] = jnp.zeros((1, 128), F32)
                BQ[l, :, 384:640] = SV[t, l, 1:2, :]
                hidden = [SV[b, l, pl.ds(2 + t, 1), :] for b in range(4)]
                for b in range(4):
                    B1[l, :, b * 128 : b * 128 + 128] = hidden[b][:, 0:128]
                for b in range(2):
                    even, odd = hidden[2 * b][:, 128:256], hidden[2 * b + 1][:, 128:256]
                    B1[l, :, 512 + b * 128 : 640 + b * 128] = jnp.where(
                        lower, even, pltpu.roll(odd, 64, 1)
                    )
            for k in range(1, 4):
                sv_copy(k).wait_send()

        def sz_copy(k):
            return remote(SMALL, SZ.at[k - 1], sz_base + k - 1, {"tensor": z_to(k)})

        def sc_copy():
            return remote(SZ.at[0], SC, sc_base, sib)

        def sq_copy(k):
            return remote(SP.at[t], SP.at[t], sq_base + k - 1, peer_dev(k))

        def small_z():
            for k in range(1, 4):
                sz_copy(k).start()

        def small_c():
            for k in range(1, 4):
                sz_copy(k).wait_recv()
            SZ[0] = SMALL[...] + SZ[0] + SZ[1] + SZ[2]
            sc_copy().start()

        def small_q():
            sc_copy().wait_recv()
            SP[t] = SZ[0] + SC[...]
            for k in range(1, 4):
                sq_copy(k).start()

        def small_end():
            for k in range(1, 4):
                remote(SC, SP.at[peer_t(k)], sq_base + k - 1, sib).wait_recv()
            z_half = lax.div(z, 2)
            upper = lax.rem(z, 2)
            for l in range(layers):
                at = slice(8 * l, 8 * l + 6)
                total = SP[0, at] + SP[1, at] + SP[2, at] + SP[3, at]
                for r in range(6):
                    shared_out[r, l : l + 1, :] = total[r : r + 1]
                line = slice(8 * l + 6, 8 * l + 7)
                split_out[0, l : l + 1, :] = SP[z, line, 0:192]
                split_out[1, l : l + 1, :] = SP[z, line, 384:576]
                line = slice(8 * l + 7, 8 * l + 8)
                for r in range(4):
                    first = SP[r, line, pl.ds(pl.multiple_of(z * 128, 128), 128)]
                    pair = SP[
                        r, line, pl.ds(pl.multiple_of(512 + z_half * 128, 128), 128)
                    ]
                    pair = jnp.where(upper == 1, pltpu.roll(pair, 64, 1), pair)
                    split_out[2 + r, l : l + 1, 0:128] = first
                    split_out[2 + r, l : l + 1, 128:192] = pair[:, 0:64]
            for k in range(1, 4):
                sz_copy(k).wait_send()
                sq_copy(k).wait_send()
            sc_copy().wait_send()

        def qkv(i, l, gathered):
            def step(k, carry):
                if gathered:
                    ag_wait(i, A, l, k)
                tp = peer_t(k)
                at = rows(tp)
                here = pl.ds(pl.multiple_of(cc * tokens + tp * shard, shard), shard)
                made = dot(A[l, at], WA[l]) + BQ[l]
                q01 = made[:, 0:128].astype(BF16) * jnp.asarray(0.125, BF16)
                qk2 = made[:, 128:256]
                q2 = qk2.astype(BF16) * jnp.asarray(0.125, BF16)
                none = jnp.zeros_like(q01)
                QC[l, tp, 0:128] = jnp.where(lower, q01, none)
                QC[l, tp, 128:256] = jnp.where(lower, none, q01)
                QC[l, tp, 256:384] = jnp.where(lower, q2, none)
                v01 = made[:, 384:512]
                v2 = jnp.where(lower, 0.0, pltpu.roll(made[:, 512:640], 64, 1))
                KV[l, 0, here] = made[:, 256:384].astype(BF16)
                KV[l, 1, here] = pltpu.roll(qk2, 64, 1).astype(BF16)
                KV[l, 2, here] = v01.astype(BF16)
                KV[l, 3, here] = v2.astype(BF16)
                VT[l, cc, 0, :, at] = jnp.transpose(v01).astype(BF16)
                VT[l, cc, 1, :, at] = jnp.transpose(v2).astype(BF16)
                return carry

            lax.fori_loop(0, 4, step, 0)
            kv_copy(l).start()
            vt_copy(l, cc).start()

        def kv_copy(l):
            at = KV.at[l, :, pl.ds(pl.multiple_of(cc * tokens, tokens), tokens)]
            return remote(at, at, kv_base[l], sib)

        def vt_copy(l, c):
            return remote(VT.at[l, c], VT.at[l, c], kv_base[l] + 1, sib)

        def kv_wait(l):
            at = KV.at[l, :, pl.ds(pl.multiple_of((1 - cc) * tokens, tokens), tokens)]
            remote(at, at, kv_base[l], sib).wait_recv()
            vt_copy(l, 1 - cc).wait_recv()

        def kv_drain(l):
            kv_copy(l).wait_send()
            vt_copy(l, cc).wait_send()

        def attend(l, hook=None):
            def weigh(scores):
                highest = jnp.max(scores, axis=0, keepdims=True)
                raised = jnp.exp(scores - highest)
                return raised.astype(BF16), 1.0 / jnp.sum(raised, axis=0, keepdims=True)

            def mix(tile, low):
                return dot(VT[l, 0, tile], low[0:tokens]) + dot(VT[l, 1, tile], low[tokens:])

            def step(s, carry):
                k = back(s)
                tp = peer_t(k)
                low, scale = weigh(dot_nt(KV[l, 0], QC[l, tp, 0:256]))
                E01[l, tp] = low
                RR[l, tp, :, 0:256] = scale
                made = mix(0, low) * scale
                both = jnp.where(top_rows, made[:, 0:128], made[:, 128:256])
                CS[k, 0:shard] = jnp.transpose(both).astype(BF16)
                low, scale = weigh(dot_nt(KV[l, 1], QC[l, tp, 256:384]))
                E2[l, tp] = low
                RR[l, tp, :, 256:384] = scale
                third = jnp.transpose(mix(1, low) * scale)
                half = shard // 2
                third = jnp.where(lower, pltpu.roll(third[0:half], 64, 1), third[half:shard])
                CS[k, shard : shard + half] = third.astype(BF16)

                @pl.when(k > 0)
                def _():
                    context_copy(l, k).start()

                if hook is not None:
                    pl.when(k == 1)(hook)
                return carry

            lax.fori_loop(0, 4, step, 0)
            CX[l, t] = CS[0]

        def context_copy(l, k):
            return remote(CS.at[k], CX.at[l, t], cx_base[l] + k - 1, peer_dev(k))

        def attended(l):
            for k in range(1, 4):
                remote(CS.at[0], CX.at[l, peer_t(k)], cx_base[l] + k - 1, sib).wait_recv()
            for b in range(4):
                CF[l, :, b * 128 : b * 128 + 128] = CX[l, b, 0:shard]
            half = shard // 2
            for b in range(2):
                even = CX[l, 2 * b, shard : shard + half].astype(F32)
                odd = CX[l, 2 * b + 1, shard : shard + half].astype(F32)
                lanes = slice(512 + b * 128, 640 + b * 128)
                first = jnp.where(lower, even, pltpu.roll(odd, 64, 1))
                second = jnp.where(lower, pltpu.roll(even, 64, 1), odd)
                CF[l, 0:half, lanes] = first.astype(BF16)
                CF[l, half:shard, lanes] = second.astype(BF16)
            for k in range(1, 4):
                context_copy(l, k).wait_send()
            return dot_nt(CF[l], WO[l])

        def turn(weight, l):
            def step(b, carry):
                at = pl.ds(pl.multiple_of(b * 128, 128), 128)
                wide = jnp.transpose(weight[l, at, :].astype(F32)).astype(BF16)
                T[0 : wide.shape[0], at] = wide
                return carry

            lax.fori_loop(0, width // 128, step, 0)

        def expand(i_ag, i_rs, l):
            def part(k):
                ag_wait(i_ag, N, l, k)
                at = rows(peer_t(k))
                f = dot(N[l, at], W1[l]) + B1[l]
                cdf = 0.5 * (1.0 + lax.erf(f * (2.0**-0.5)))
                slope = cdf + f * jnp.exp(-0.5 * f * f) * ((2.0 * math.pi) ** -0.5)
                H[l, at] = (f * cdf).astype(BF16)
                DG[l, at] = slope.astype(BF16)
                return dot(H[l, at], T[...])

            rs_loop(i_rs, forth, part)

        def shrink_back(i_ag, i_rs, l, gathered):
            def part(k):
                if gathered:
                    ag_wait(i_ag, GY, l, k)
                at = rows(peer_t(k))
                g = dot(GY[l, at], W2[l]) * DG[l, at].astype(F32)
                GF[at, :] = g.astype(BF16)
                return dot(GF[at, :], T[...])

            rs_loop(i_rs, forth, part)

        def context_grad_copy(l, k):
            return remote(CS.at[k], GC.at[l, t], gc_base[l] + k - 1, peer_dev(k))

        def context_grads(l, value):
            GO[l] = value
            made = dot(value, WO[l])
            half = shard // 2
            for b in range(4):
                CX[l, b, 0:shard] = made[:, b * 128 : b * 128 + 128].astype(BF16)
                pair = made[:, 512 + (b // 2) * 128 : 640 + (b // 2) * 128]
                first, second = pair[0:half], pair[half:shard]
                if b % 2 == 0:
                    both = jnp.where(lower, first, pltpu.roll(second, 64, 1))
                else:
                    both = jnp.where(lower, pltpu.roll(first, 64, 1), second)
                CX[l, b, shard : shard + half] = both.astype(BF16)
            for k in (3, 1, 2):
                CS[k] = CX[l, peer_t(k)]
                context_grad_copy(l, k).start()
            GC[l, t] = CX[l, t]

        def attend_back(l, hook):
            GKV[...] = jnp.zeros_like(GKV)
            for tile in range(2):
                for half in range(2):
                    keys = KV[l, tile, half * tokens : (half + 1) * tokens]
                    VT[0, half, tile] = jnp.transpose(keys.astype(F32)).astype(BF16)

            def step(k, carry):
                tp = peer_t(k)
                at = rows(tp)

                @pl.when(k > 0)
                def _():
                    remote(
                        CS.at[0], GC.at[l, tp], gc_base[l] + k - 1, sib
                    ).wait_recv()

                pl.when(k == 1)(hook)
                scale = RR[l, tp]
                r01, r2 = scale[:, 0:256], scale[:, 256:384]
                spread = jnp.where(top_rows, scale[:, 0:128], scale[:, 128:256])
                by_row = jnp.transpose(spread)
                by_row2 = jnp.transpose(jnp.where(top_rows, 0.0, r2))
                c01 = (GC[l, tp, 0:shard].astype(F32) * by_row).astype(BF16)
                third = GC[l, tp, shard : shard + shard // 2].astype(F32)
                third = jnp.concatenate([pltpu.roll(third, 64, 1), third], axis=0)
                c2 = (third * by_row2).astype(BF16)
                none = jnp.zeros_like(c01)
                c01 = jnp.concatenate(
                    [jnp.where(lower, c01, none), jnp.where(lower, none, c01)], axis=0
                )
                made = []
                for tile, low_ref, scale, grad, lanes in (
                    (0, E01, r01, c01, slice(0, 256)),
                    (1, E2, r2, c2, slice(256, 384)),
                ):
                    gp = dot_nt(KV[l, 2 + tile], grad)
                    low = low_ref[l, tp]
                    e = low.astype(F32)
                    inner = scale * jnp.sum(e * gp, axis=0, keepdims=True)
                    gs = (e * (gp - inner)).astype(BF16)
                    GKV[tile] += dot(gs, QC[l, tp, lanes])
                    GKV[2 + tile] += dot(low, grad)
                    made.append(dot(VT[0, 0, tile], gs[0:tokens]) + dot(VT[0, 1, tile], gs[tokens:]))
                both = jnp.where(top_rows, made[0][:, 0:128], made[0][:, 128:256])
                GQ[at, 0:128] = (0.125 * jnp.transpose(both)).astype(BF16)
                third = jnp.where(lower, 0.125 * jnp.transpose(made[1]), 0.0)
                GQ[at, 128:256] = third.astype(BF16)
                return carry

            lax.fori_loop(0, 4, step, 0)
            other = pl.ds(pl.multiple_of((1 - cc) * tokens, tokens), tokens)
            for tile in range(4):
                KVS[tile] = GKV[tile, other].astype(BF16)
            gkv_copy(l).start()
            for k in range(1, 4):
                context_grad_copy(l, k).wait_send()

        def gkv_copy(l):
            return remote(KVS, KVR.at[l], gkv_base[l], sib)

        def heads_back(i, l):
            gkv_copy(l).wait_recv()
            gkv_copy(l).wait_send()

            def part(k):
                at = rows(peer_t(k))
                here = pl.ds(pl.multiple_of(cc * tokens + peer_t(k) * shard, shard), shard)
                k01, k2, v01, v2 = (
                    GKV[tile, here] + KVR[l, tile, at].astype(F32) for tile in range(4)
                )
                G[at, 0:128] = GQ[at, 0:128]
                G[at, 128:256] = (
                    GQ[at, 128:256].astype(F32) + pltpu.roll(k2, 64, 1)
                ).astype(BF16)
                G[at, 256:384] = k01.astype(BF16)
                G[at, 384:512] = v01.astype(BF16)
                G[at, 512:640] = pltpu.roll(v2, 64, 1).astype(BF16)
                return dot(G[at, :], T[0:640, :])

            rs_loop(i, back, part)

        spread_start(frames, X0, 0)
        att_b_start(0)
        att_a_piece(0, 0)
        biases_start()
        mlp_a_start(0)
        for p in range(4):
            spread_pass(X0, 0, p)
        for p in range(4):
            spread_wait(frames, X0, 0, p)
        att_a_first(0)

        def first_norm(k, carry):
            at = rows(k)
            hat, inverse = norm_parts(X0[at, :].astype(F32))
            A[0, at] = (hat * row(0, 0) + row(0, 1)).astype(BF16)
            return carry

        lax.fori_loop(0, 4, first_norm, 0)
        XS[0] = X0[rows(t), :].astype(F32)
        att_a_rest(0)
        out_b_start(0)
        mlp_b_start(0)
        biases_ready()
        att_c_start(0)
        att_ready(0)
        spread_start(cot, GY.at[top], 1)
        for l in range(layers):
            qkv(4 * l + 3, l, l > 0)
            out_a_start(l)
            kv_wait(l)
            if l == 0:
                for p in range(4):
                    spread_pass(GY.at[top], 1, p)
            attend(l, (lambda: mlp_pass(0)) if l == 0 else None)
            out_c_start(l)
            if l > 0:
                mlp_pass(l)
            out_ready(l)
            between = XS[l] + attended(l) + row(l, 2)
            MS[l] = between
            hat, inverse = norm_parts(between)
            ag_start(4 * l, N, l, (hat * row(l, 3) + row(l, 4)).astype(BF16))
            mlp_c_start(l)
            mlp_ready(l)
            if l + 1 < layers:
                att_b_start(l + 1)
                out_b_start(l + 1)
            turn(W2, l)
            expand(4 * l, l, l)
            if l + 1 < layers:
                mlp_a_start(l + 1)
                att_a_piece(l + 1, 0)
                att_a_first(l + 1)
                att_a_rest(l + 1)
                mlp_b_start(l + 1)
                total = rs_finish(l)
                stream = MS[l] + total + row(l, 5)
                XS[l + 1] = stream
                hat, inverse = norm_parts(stream)
                normed = (hat * row(l + 1, 0) + row(l + 1, 1)).astype(BF16)
                ag_start(4 * l + 7, A, l + 1, normed)
                att_c_start(l + 1)
                att_ready(l + 1)
            else:
                turn(W1, l)
                total = rs_finish(l)
                out_start(0, MS[l] + total + row(l, 5))

        spread_drain(frames, X0, 0)
        for l in range(layers):
            kv_drain(l)
        for p in range(4):
            spread_wait(cot, GY.at[top], 1, p)
        GS[...] = GY[top, rows(t)].astype(F32)
        rs_next = layers
        for l in reversed(range(layers)):
            shrink_back(4 * l + 2, rs_next, l, l < top)
            mlp_grads(l)
            mlp_grad_b(l)
            mlp_sum[l][0]()
            grad = GS[...]
            SMALL[8 * l + 5 : 8 * l + 6, :] = jnp.sum(grad, axis=0, keepdims=True)
            gn = rs_finish(rs_next)
            rs_next += 1
            hat, inverse = norm_parts(MS[l])
            gm = grad + norm_back(gn, hat, inverse, row(l, 3))
            context_grads(l, gm.astype(BF16))
            GS[...] = gm
            SMALL[8 * l + 3 : 8 * l + 4, :] = jnp.sum(gn * hat, axis=0, keepdims=True)
            SMALL[8 * l + 4 : 8 * l + 5, :] = jnp.sum(gn, axis=0, keepdims=True)
            SMALL[8 * l + 2 : 8 * l + 3, :] = jnp.sum(gm, axis=0, keepdims=True)
            if l < top:
                att_grad_a(l + 1)
            out_grads(l)

            def hook(l=l):
                if l == top:
                    out_z[0][1]()
                    out_forward(0, (0, 2))
                out_grad_a(l)

            attend_back(l, hook)
            if l < top:
                att_grad_b(l + 1)
            turn(WA, l)
            heads_back(rs_next, l)
            mlp_sum[l][1]()
            att_grads(l)
            out_grad_b(l)
            if l < top:
                att_sum[l + 1][1]()
            if l == 0:
                att_grad_a(l)
            gn = rs_finish(rs_next)
            rs_next += 1
            hat, inverse = norm_parts(XS[l])
            gx = GS[...] + norm_back(gn, hat, inverse, row(l, 0))
            if l > 0:
                ag_start(4 * l - 2, GY, l - 1, gx.astype(BF16))
                GS[...] = gx
            SMALL[8 * l : 8 * l + 1, :] = jnp.sum(gn * hat, axis=0, keepdims=True)
            SMALL[8 * l + 1 : 8 * l + 2, :] = jnp.sum(gn, axis=0, keepdims=True)
            if l == 0:
                small_z()
                out_start(1, gx)
                out_forward(1, (0,))
            else:
                turn(W1, l - 1)
                out_grad_end(l)
        small_c()
        if layers > 1:
            mlp_grad_a(1)
        att_grad_b(0)
        out_forward(0, (1, 3))
        if layers > 1:
            mlp_grad_end(1)
        mlp_grad_a(0)
        small_q()
        out_z[1][1]()
        out_forward(1, (2,))
        att_sum[0][1]()
        out_forward(1, (1, 3))
        if layers > 1:
            att_grad_end(1)
        mlp_grad_end(0)
        out_grad_end(0)
        small_end()
        out_finish(0, enc)
        att_grad_end(0)
        out_finish(1, xg)

        spread_drain(cot, GY.at[top], 1)
        for l in range(layers):
            att_drain(l)
            ag_drain(4 * l, N, l)
            out_drain(l)
            if l < top:
                ag_drain(4 * l + 2, GY, l)
            if l > 0:
                ag_drain(4 * l + 3, A, l)

    return kernel


def fused_step(frames, cot, hw, mw, wm, shared, sv):
    layers, rows_of, _ = mw.shape
    tokens, width = frames.shape
    shard = tokens // 4
    numbers = Numbers()
    kernel = make_kernel(layers, tokens, width, numbers)
    two = 2 * tokens
    v = pltpu.VMEM
    scratch = [
        v((layers, shard, width), F32),
        v((layers, shard, width), F32),
        v((layers, tokens, width), BF16),
        v((layers, tokens, width), BF16),
        v((layers, shard, width), BF16),
        v((layers, tokens, width), BF16),
        v((shard, width), F32),
        v((layers, width, 640), BF16),
        v((layers, width, width), BF16),
        v((layers, width, width), BF16),
        v((layers, width, width), BF16),
        v((width, width), BF16),
        v((layers, 4, rows_of, 640), BF16),
        v((layers, 4, rows_of, 256), BF16),
        v((layers, 2, 4, 4, rows_of, width // 2), BF16),
        v((layers, 4, 3 * shard, 128), BF16),
        v((layers, 4, two, 128), BF16),
        v((layers, 2, 2, 128, tokens), BF16),
        v((layers, 4, two, 2 * shard), BF16),
        v((layers, 4, two, shard), BF16),
        v((layers, 4, 1, 3 * shard), F32),
        v((4, 3 * shard // 2, 128), BF16),
        v((layers, 4, 3 * shard // 2, 128), BF16),
        v((layers, shard, width), BF16),
        v((layers, 4, 3 * shard // 2, 128), BF16),
        v((layers, tokens, width), BF16),
        v((layers, tokens, width), BF16),
        v((tokens, width), BF16),
        v((tokens, 256), BF16),
        v((tokens, 640), BF16),
        v((4, two, 128), F32),
        v((4, tokens, 128), BF16),
        v((layers, 4, tokens, 128), BF16),
        v((shard, width), F32),
        v((4, shard, width), BF16),
        v((2, 3, shard, width), BF16),
        v((4, 4, rows_of, width // 2), BF16),
        v((layers, 3, 4, rows_of, width // 2), BF16),
        v((4, rows_of, width // 2), BF16),
        v((layers, 4, rows_of, width // 2), BF16),
        v((layers, 4, rows_of, width // 2), BF16),
        v((layers, rows_of, 640), BF16),
        v((2, 4, rows_of, 640), BF16),
        v((4, rows_of, 640), BF16),
        v((layers, 4, rows_of, 640), BF16),
        v((layers, 3, rows_of, 640), BF16),
        v((2, 4, rows_of, width), BF16),
        v((4, rows_of, width), BF16),
        v((layers, 3, rows_of, width), BF16),
        v((4, rows_of, 256), BF16),
        v((layers, 3, rows_of, 256), BF16),
        v((2, 4, shard, width), BF16),
        v((4, layers, 8, 256), F32),
        v((layers, 1, 640), F32),
        v((layers, 1, width), F32),
        v((8 * layers, width), F32),
        v((3, 8 * layers, width), F32),
        v((8 * layers, width), F32),
        v((4, 8 * layers, width), F32),
        pltpu.SemaphoreType.DMA((numbers.count,)),
        pltpu.SemaphoreType.DMA((numbers.count,)),
        pltpu.SemaphoreType.DMA((4,)),
    ]
    inside = pl.BlockSpec(memory_space=pltpu.VMEM)
    outside = pl.BlockSpec(memory_space=pl.ANY)
    return pl.pallas_call(
        kernel,
        out_shape=(
            jax.ShapeDtypeStruct((4, shard, width), BF16),
            jax.ShapeDtypeStruct((4, shard, width), BF16),
            jax.ShapeDtypeStruct((layers, 3, rows_of, width // 4), BF16),
            jax.ShapeDtypeStruct((layers, rows_of, width // 4), BF16),
            jax.ShapeDtypeStruct((layers, 4, rows_of, width // 2), BF16),
            jax.ShapeDtypeStruct((6, layers, width), F32),
            jax.ShapeDtypeStruct((6, layers, width // 4), F32),
        ),
        in_specs=[outside, outside] + [inside] * 5,
        out_specs=(outside, outside) + (inside,) * 5,
        scratch_shapes=scratch,
        compiler_params=pltpu.CompilerParams(
            collective_id=0, has_side_effects=True, vmem_limit_bytes=63 * 1024 * 1024
        ),
    )(frames, cot, hw, mw, wm, shared, sv)


def adam_update(weight, gradient, first_moment, second, step_rate):
    first_new = beta_one * first_moment + (1.0 - beta_one) * gradient
    second_new = beta_two * second + (1.0 - beta_two) * gradient * gradient
    bias_one = 1.0 - beta_one**STEP
    bias_two = 1.0 - beta_two**STEP
    direction = first_new / bias_one / (jnp.sqrt(second_new / bias_two) + adam_epsilon)
    return (second_new, weight - step_rate * (direction + weight_decay * weight))


RATES = (0.1, 0.1, 0.1, 0.1, 2.0, 0.5)


def finish_kernel(*refs):
    enc, xg, pairs = refs[0:3]
    outs = refs[25:]
    groups, at = [], 3
    for i in range(6):
        packed = i in (2, 3)
        grad = (outs[2 + 3 * i],) if packed else (refs[at],)
        at += 0 if packed else 1
        groups.append(grad + tuple(refs[at : at + 3]))
        at += 3
    for r in range(4):
        total = pairs[0, r].astype(F32)
        third = pltpu.roll(total[:, 128:256], 64, 1)
        outs[8][0, :, r, :] = total[:, 0:192]
        outs[11][0, :, r, 0:128] = total[:, 256:384]
        outs[11][0, :, r, 128:192] = third[:, 0:64]
    outs[0][...] = enc[...].astype(F32)
    outs[1][...] = xg[...].astype(F32)
    for i, (grad, weight, first, second) in enumerate(groups):
        g = grad[...].astype(F32)
        renewed, updated = adam_update(weight[...], g, first[...], second[...], RATES[i])
        if i not in (2, 3):
            outs[2 + 3 * i][...] = g
        outs[3 + 3 * i][...] = renewed
        outs[4 + 3 * i][...] = updated


def finish(enc, xg, pairs, groups):
    layers, _, rows_of, wide = groups[0][0].shape
    tokens, width = enc.shape
    cut = 2 if rows_of % 16 == 0 else 1
    steps = layers * cut
    part = rows_of // cut
    stream = pl.BlockSpec((tokens // steps, width), lambda l, h: (cut * l + h, 0))
    heads = pl.BlockSpec((1, 3, part, wide), lambda l, h: (l, 0, h, 0))
    flat = pl.BlockSpec((1, part, wide), lambda l, h: (l, h, 0))
    grid = pl.BlockSpec((1, part, 4, wide), lambda l, h: (l, h, 0, 0))
    shared = pl.BlockSpec((6, layers, width), lambda l, h: (0, 0, 0))
    split = pl.BlockSpec((6, layers, wide), lambda l, h: (0, 0, 0))
    kinds = (heads, flat, grid, grid, shared, split)
    both = pl.BlockSpec((1, 4, part, 2 * wide), lambda l, h: (l, 0, h, 0))
    shapes = [jax.ShapeDtypeStruct((tokens, width), F32)] * 2
    out_specs = [stream, stream]
    for kind, group in zip(kinds, groups):
        shapes += [jax.ShapeDtypeStruct(group[-1].shape, F32)] * 3
        out_specs += [kind] * 3
    return pl.pallas_call(
        finish_kernel,
        grid=(layers, cut),
        out_shape=shapes,
        in_specs=[stream, stream, both]
        + [kind for kind, group in zip(kinds, groups) for _ in group],
        out_specs=out_specs,
        compiler_params=pltpu.CompilerParams(
            dimension_semantics=("arbitrary", "arbitrary"),
            vmem_limit_bytes=63 * 1024 * 1024,
        ),
    )(enc, xg, pairs, *[v for group in groups for v in group])


def shards(
    frames, cotangent, heads_weight, merge_weight, expand_weight, shrink_weight,
    shared_vectors, split_vectors,
    heads_first, heads_second, merge_first, merge_second, expand_first, expand_second,
    shrink_first, shrink_second, shared_first, shared_second, split_first, split_second,
):
    groups = lax.axis_size("dp") // 4
    width = frames.shape[-1]
    dp_group = [[lo + 4 * h for h in range(groups)] for lo in range(4)]

    def to_kernel(v):
        if groups == 1:
            return v
        part = v.reshape(v.shape[:-1] + (groups, 8, width // (8 * groups)))
        return jnp.swapaxes(part, -3, -2).reshape(v.shape)

    def from_kernel(v):
        if groups == 1:
            return v
        part = v.reshape(v.shape[:-1] + (8, groups, width // (8 * groups)))
        return jnp.swapaxes(part, -3, -2).reshape(v.shape)

    def widen(v, axis):
        if groups == 1:
            return v
        return lax.all_gather(
            v, "dp", axis=axis, tiled=True, axis_index_groups=dp_group
        )

    def narrow(v, axis):
        if groups == 1:
            return v
        return lax.psum_scatter(
            v.astype(BF16),
            "dp",
            scatter_dimension=axis,
            tiled=True,
            axis_index_groups=dp_group,
        ).astype(F32)

    e = jnp.swapaxes(expand_weight.astype(BF16), 1, 2)
    s = jnp.swapaxes(shrink_weight.astype(BF16), 1, 2)
    wm = jnp.concatenate([e, s[..., 128:], s[..., :128]], axis=-1)
    wm = widen(wm, 2)
    hw, mw = jnp.swapaxes(heads_weight, 1, 2), merge_weight
    if groups > 1:
        hw = widen(hw.astype(BF16), 2).astype(F32)
        mw = widen(mw.astype(BF16), 1).astype(F32)

    enc, xg, heads_grad, merge_grad, pairs, shared_grad, split_grad = (
        fused_step(
            to_kernel(frames[0]),
            to_kernel(cotangent[0]),
            hw,
            mw,
            wm,
            jnp.swapaxes(to_kernel(shared_vectors), 0, 1),
            jnp.swapaxes(split_vectors, 0, 1),
        )
    )
    enc, xg = (from_kernel(v.reshape(frames.shape[1:])) for v in (enc, xg))
    heads_grad = narrow(heads_grad, 2)
    merge_grad = narrow(merge_grad, 1)
    pairs = narrow(pairs, 2)
    shared_grad = from_kernel(shared_grad)
    if groups > 1:
        shared_grad = lax.psum(shared_grad, "dp", axis_index_groups=dp_group)
        split_grad = lax.psum(split_grad, "dp", axis_index_groups=dp_group)

    def turned(v):
        return jnp.swapaxes(v, 1, 2)

    def lined(v):
        return jnp.swapaxes(v, 0, 1)

    def same(v):
        return v

    table = (
        (turned, (heads_grad,), heads_weight, heads_first, heads_second),
        (same, (merge_grad,), merge_weight, merge_first, merge_second),
        (same, (), expand_weight, expand_first, expand_second),
        (same, (), shrink_weight, shrink_first, shrink_second),
        (lined, (shared_grad,), shared_vectors, shared_first, shared_second),
        (lined, (split_grad,), split_vectors, split_first, split_second),
    )
    groups_in = [g + tuple(view(v) for v in rest) for view, g, *rest in table]
    done = finish(enc, xg, pairs, groups_in)
    out = [done[0][None], done[1][None]]
    for i, (view, *_) in enumerate(table):
        out += [view(v) for v in done[2 + 3 * i : 5 + 3 * i]]
    return tuple(out)


def solution(mesh):
    rows = ("dp", "seq")
    stream = P("dp", "seq", None)
    wide = P(None, rows, None, "tensor")
    flat = P(None, rows, "tensor")
    split = P(None, None, "tensor")
    return jax.shard_map(
        shards,
        mesh=mesh,
        in_specs=(
            stream, stream, wide, flat, wide, wide, P(), split,
            wide, wide, flat, flat, wide, wide, wide, wide, P(), P(), split, split,
        ),
        out_specs=(stream, stream)
        + (wide,) * 3 + (flat,) * 3 + (wide,) * 6 + (P(),) * 3 + (split,) * 3,
        check_vma=False,
    )
```

```python
import math

import jax
import jax.numpy as jnp
from jax import lax
from jax.experimental import pallas as pl
from jax.experimental.pallas import tpu as pltpu
from jax.sharding import PartitionSpec as P

HEAD_DIM = 64
STEP = 10

beta_one = 0.9
beta_two = 0.999
adam_epsilon = 1e-08
weight_decay = 0.01
norm_epsilon = 1e-05

MESH = pl.DeviceIdType.MESH
F32 = jnp.float32
BF16 = jnp.bfloat16


def dot(a, b):
    return lax.dot_general(a, b, (((1,), (0,)), ((), ())), preferred_element_type=F32)


def dot_nt(a, b):
    return lax.dot_general(a, b, (((1,), (1,)), ((), ())), preferred_element_type=F32)


def dot_tn(a, b):
    return lax.dot_general(a, b, (((0,), (0,)), ((), ())), preferred_element_type=F32)


def norm_parts(values):
    centre = values - jnp.mean(values, axis=-1, keepdims=True)
    spread = jnp.mean(centre * centre, axis=-1, keepdims=True)
    inverse = lax.rsqrt(spread + norm_epsilon)
    return centre * inverse, inverse


def norm_back(grad, hat, inverse, gain):
    scaled = grad * gain
    first = jnp.mean(scaled, axis=-1, keepdims=True)
    second = jnp.mean(scaled * hat, axis=-1, keepdims=True)
    return inverse * (scaled - first - hat * second)


class Numbers:
    def __init__(self):
        self.count = 0

    def take(self, n):
        base = self.count
        self.count += n
        return base


def make_kernel(layers, tokens, width, numbers):
    shard = tokens // 4
    rows_of = 96
    take = numbers.take
    rs_base = [take(3) for _ in range(3 * layers)]
    ag_base = [take(4) for _ in range(4 * layers)]
    sp_base = [take(16), take(16)]
    sv_base, sz_base, sc_base, sq_base = take(3), take(3), take(1), take(3)
    cx_base = [take(3) for _ in range(layers)]
    gc_base = [take(3) for _ in range(layers)]
    ob, oa, oc = ([take(n) for _ in range(layers)] for n in (3, 3, 4))
    goc, goa, gob = ([take(n) for _ in range(layers)] for n in (1, 3, 3))
    kv_base = [take(2) for _ in range(layers)]
    gkv_base = [take(1) for _ in range(layers)]
    ab, aa, ac = ([take(n) for _ in range(layers)] for n in (4, 3, 4))
    ma, mb, mc = ([take(n) for _ in range(layers)] for n in (3, 4, 4))
    gac, gaa, gab = ([take(n) for _ in range(layers)] for n in (1, 3, 4))
    gmc, gmb, gma = ([take(n) for _ in range(layers)] for n in (1, 4, 3))
    oz = [take(4) for _ in range(2)]
    op = [take(4) for _ in range(2)]
    top = layers - 1

    def kernel(
        frames, cot, hw, mw, wm, shared, sv,
        enc, xg, gh_out, go_out, gm_out, shared_out, split_out,
        XS, MS, A, N, GO, GY, GS,
        WA, WO, W1, W2, T, GA, GB, GM,
        QC, KV, VT, E01, E2, RR, CS, CX, CF, GC, H, DG, GF, GQ, G,
        GKV, KVS, KVR,
        OWN, RSS, RSR,
        CM, BM, TM, UM,
        FM, FA, SA, CA, RA, RB, SO, CO, RO, TO, RP,
        EZ, SV, BQ, B1, SMALL, SZ, SC, SP,
        ssem, rsem, lsem,
    ):
        dp = lax.axis_index("dp")
        y = lax.axis_index("seq")
        z = lax.axis_index("tensor")
        hi = lax.div(dp, 4)
        lo = lax.rem(dp, 4)
        xx = lax.div(lo, 2)
        cc = lax.rem(lo, 2)
        t = 2 * xx + y

        def flip(bit, by):
            return bit + by - 2 * bit * by

        def peer(k):
            if isinstance(k, int):
                kx, ky = k // 2, k % 2
            else:
                kx, ky = lax.div(k, 2), lax.rem(k, 2)
            return flip(xx, kx), flip(y, ky)

        def peer_t(k):
            px, py = peer(k)
            return 2 * px + py

        def peer_dev(k):
            px, py = peer(k)
            return {"dp": 4 * hi + 2 * px + cc, "seq": py}

        def peer_j(k):
            px, py = peer(k)
            return 4 * px + 2 * cc + py

        my_j = 4 * xx + 2 * cc + y
        sib = {"dp": dp + 1 - 2 * cc}

        def z_to(k):
            return lax.rem(z + k, 4)

        def z_from(k):
            return lax.rem(z + 4 - k, 4)

        middle = jnp.logical_or(z == 1, z == 2)

        def z_near(k, act):
            if k == 2:
                act()
            else:
                pl.when(z != (3 if k == 1 else 0))(act)

        def z_far(k, act):
            pl.when(z == (3 if k == 1 else 0))(act)

        def z_come(k, act):
            pl.when(z != (0 if k == 1 else 3))(act)

        def gather_z(slot, base):
            def copy(k):
                return remote(slot(z), slot(z), base + k - 1, {"tensor": z_to(k)})

            def relay():
                far = slot(z_from(2))
                return remote(
                    far, far, base + 2 * (z - 1), {"tensor": 3 * (z - 1)}, send=base + 3
                )

            def wait(k):
                remote(slot(z), slot(z_from(k)), base + k - 1, sib).wait_recv()

            def start():
                for k in (2, 1, 3):
                    z_near(k, lambda k=k: copy(k).start())

            def pass_on():
                wait(2)
                pl.when(middle)(lambda: relay().start())

            def drain():
                for k in (2, 1, 3):
                    z_near(k, lambda k=k: copy(k).wait_send())
                pl.when(middle)(lambda: relay().wait_send())

            return start, pass_on, wait, drain

        def sum_z(part, far, landing, base):
            def copy(k):
                return remote(part(z_to(k)), landing(k), base + k - 1, {"tensor": z_to(k)})

            def far_copy():
                end = lax.div(z, 3)
                return remote(part(3 - z), far, base + 3, {"tensor": 1 + end})

            def start_far():
                pl.when(jnp.logical_not(middle))(lambda: far_copy().start())

            def start():
                for k in (1, 3):
                    z_near(k, lambda k=k: copy(k).start())
                    at = landing(k)

                    @pl.when(z == (0 if k == 1 else 3))
                    def _(at=at):
                        at[...] = jnp.zeros(at.shape, BF16)

                pl.when(jnp.logical_not(middle))(lambda: copy(2).start())

            def combine():
                @pl.when(middle)
                def _():
                    far_copy().wait_recv()
                    at = part(z_to(2))
                    at[...] = (at[...].astype(F32) + far[...].astype(F32)).astype(BF16)
                    copy(2).start()

            def wait():
                copy(2).wait_recv()
                for k in (1, 3):
                    z_come(k, lambda k=k: copy(k).wait_recv())

            def drain():
                copy(2).wait_send()
                for k in (1, 3):
                    z_near(k, lambda k=k: copy(k).wait_send())
                pl.when(jnp.logical_not(middle))(lambda: far_copy().wait_send())

            return start, combine, wait, drain, start_far

        def remote(src, dst, number, dev, send=None):
            send = number if send is None else send
            return pltpu.make_async_remote_copy(
                src_ref=src,
                dst_ref=dst,
                send_sem=ssem.at[send],
                recv_sem=rsem.at[number],
                device_id=dev,
                device_id_type=MESH,
            )

        def rows(k_t):
            return pl.ds(pl.multiple_of(k_t * shard, shard), shard)

        def block(j):
            return pl.ds(pl.multiple_of(j * rows_of, rows_of), rows_of)

        X0 = GF
        lower = lax.broadcasted_iota(jnp.int32, (1, 128), 1) < 64
        top_rows = lax.broadcasted_iota(jnp.int32, (128, 1), 0) < 64

        barrier = pltpu.get_barrier_semaphore()
        for k in range(1, 8):
            dev = {
                "dp": 4 * hi + 2 * flip(xx, k // 4) + flip(cc, (k // 2) % 2),
                "seq": flip(y, k % 2),
            }
            pl.semaphore_signal(barrier, inc=1, device_id=dev, device_id_type=MESH)
        for k in range(1, 4):
            pl.semaphore_signal(
                barrier, inc=1, device_id={"tensor": z_to(k)}, device_id_type=MESH
            )
        pl.semaphore_wait(barrier, 10)

        xs = lax.div(z, 2)
        source = jnp.logical_and(lo == z, y == cc)
        relay = jnp.logical_and(xx != xs, y == cc)
        relay_dev = {"dp": dp, "seq": 1 - y}

        def piece(p):
            return pl.ds(p * shard, shard)

        def spread_each(src, dst, i, act, act_own):
            @pl.when(lo == z)
            def _():
                for p in range(4):
                    for d, (dx, dy) in enumerate(((1, 0), (0, 1), (0, 0))):
                        same = jnp.logical_and(cc == y, (dx, dy) == (0, 0))
                        dev = {"dp": 4 * hi + 2 * flip(xx, dx) + y, "seq": flip(y, dy)}

                        @pl.when(jnp.logical_not(same))
                        def _(p=p, d=d, dev=dev):
                            act(
                                remote(
                                    src.at[piece(p)],
                                    dst.at[piece(p)],
                                    sp_base[i] + p,
                                    dev,
                                    send=sp_base[i] + 4 + 3 * p + d,
                                )
                            )

            if act_own is not None:

                @pl.when(source)
                def _():
                    act_own(pltpu.make_async_copy(src, dst, lsem.at[i]))

        def spread_start(src, dst, i):
            spread_each(src, dst, i, lambda c: c.start(), lambda c: c.start())

        def relay_copy(dst, i, p):
            return remote(
                dst.at[piece(p)],
                dst.at[piece(p)],
                sp_base[i] + p,
                relay_dev,
                send=sp_base[i] + 4 + p,
            )

        def spread_pass(dst, i, p):
            @pl.when(relay)
            def _():
                relay_copy(dst, i, p).wait_recv()
                relay_copy(dst, i, p).start()

        def spread_wait(src, dst, i, p):
            if p == 0:

                @pl.when(source)
                def _():
                    pltpu.make_async_copy(src, dst, lsem.at[i]).wait()

            @pl.when(jnp.logical_not(jnp.logical_or(source, relay)))
            def _():
                relay_copy(dst, i, p).wait_recv()

        def spread_drain(src, dst, i):
            spread_each(src, dst, i, lambda c: c.wait_send(), None)

            @pl.when(relay)
            def _():
                for p in range(4):
                    relay_copy(dst, i, p).wait_send()

        att_z = [gather_z(lambda b, l=l: GA.at[l, b], ab[l]) for l in range(layers)]
        mlp_z = [gather_z(lambda b, l=l: GM.at[l, cc, b], mb[l]) for l in range(layers)]
        out_z = [gather_z(lambda b, i=i: EZ.at[i, b], oz[i]) for i in range(2)]

        def att_b_start(l):
            q, k, v = (hw[l, i].astype(BF16) for i in range(3))
            GA[l, z, :, 0:128] = q[:, 0:128]
            GA[l, z, :, 128:256] = jnp.concatenate([q[:, 128:192], k[:, 128:192]], axis=1)
            GA[l, z, :, 256:384] = k[:, 0:128]
            GA[l, z, :, 384:512] = v[:, 0:128]
            third = v[:, 128:192]
            GA[l, z, :, 512:640] = jnp.concatenate([third, jnp.zeros_like(third)], axis=1)
            att_z[l][0]()

        def att_a_copy(l, b):
            bx, by = lax.div(b, 2), lax.rem(b, 2)
            k = 2 * flip(xx, bx) + flip(y, by)
            return remote(
                GA.at[l, b],
                WA.at[l, block(my_j)],
                aa[l] + k - 1,
                {"dp": 4 * hi + 2 * bx + cc, "seq": by},
            )

        def att_a_piece(l, zk):
            b = z_from(zk)

            @pl.when(b != t)
            def _():
                att_a_copy(l, b).start()

            @pl.when(b == t)
            def _():
                WA[l, block(my_j)] = GA[l, t]

        def att_a_first(l):
            att_z[l][1]()
            att_a_piece(l, 2)

        def att_a_rest(l):
            for k in (1, 3):
                att_z[l][2](k)
                att_a_piece(l, k)

        def att_c_copy(l, k):
            at = WA.at[l, block(peer_j(k))]
            return remote(at, at, ac[l] + k, sib)

        def att_c_start(l):
            att_c_copy(l, 0).start()
            for k in range(1, 4):
                remote(
                    GA.at[l, 0], WA.at[l, block(peer_j(k))], aa[l] + k - 1, sib
                ).wait_recv()
                att_c_copy(l, k).start()

        def att_ready(l):
            for k in range(4):
                px, py = peer(k)
                at = WA.at[l, block(4 * px + 2 * (1 - cc) + py)]
                remote(at, at, ac[l] + k, sib).wait_recv()

        def att_drain(l):
            att_z[l][3]()
            for k in range(1, 4):
                att_a_copy(l, peer_t(k)).wait_send()
            for k in range(4):
                att_c_copy(l, k).wait_send()

        def out_b_copy(l, k):
            return remote(GB.at[l, z], GB.at[l, z], ob[l] + k - 1, {"tensor": z_to(k)})

        def out_b_start(l):
            own = mw[l].astype(BF16)
            third = own[:, 128:192]
            none = jnp.zeros_like(third)
            odd = lax.rem(z, 2) == 1
            GB[l, z, :, 0:128] = own[:, 0:128]
            GB[l, z, :, 128:256] = jnp.where(
                odd,
                jnp.concatenate([none, third], axis=1),
                jnp.concatenate([third, none], axis=1),
            )
            for k in range(1, 4):
                out_b_copy(l, k).start()

        def out_a_copy(l, k):
            at = WO.at[l, block(my_j)]
            return remote(at, at, oa[l] + k - 1, peer_dev(k))

        def out_a_start(l):
            for k in range(1, 4):
                remote(GB.at[l, z], GB.at[l, z_from(k)], ob[l] + k - 1, sib).wait_recv()
            at = block(my_j)
            for b in range(4):
                WO[l, at, b * 128 : b * 128 + 128] = GB[l, b, :, 0:128]
            for b in range(2):
                pair = GB[l, 2 * b, :, 128:256] + GB[l, 2 * b + 1, :, 128:256]
                WO[l, at, 512 + b * 128 : 640 + b * 128] = pair
            for k in range(1, 4):
                out_a_copy(l, k).start()

        def out_c_copy(l, k):
            at = WO.at[l, block(peer_j(k))]
            return remote(at, at, oc[l] + k, sib)

        def out_c_start(l):
            out_c_copy(l, 0).start()
            for k in range(1, 4):
                at = WO.at[l, block(peer_j(k))]
                remote(at, at, oa[l] + k - 1, sib).wait_recv()
                out_c_copy(l, k).start()

        def out_ready(l):
            for k in range(4):
                px, py = peer(k)
                at = WO.at[l, block(4 * px + 2 * (1 - cc) + py)]
                remote(at, at, oc[l] + k, sib).wait_recv()

        def out_drain(l):
            for k in range(1, 4):
                out_b_copy(l, k).wait_send()
                out_a_copy(l, k).wait_send()
            for k in range(4):
                out_c_copy(l, k).wait_send()

        def mlp_a_copy(l, k):
            return remote(
                wm.at[l, peer_t(k)], GM.at[l, cc, z, t], ma[l] + k - 1, peer_dev(k)
            )

        def mlp_a_start(l):
            for k in range(1, 4):
                mlp_a_copy(l, k).start()
            GM[l, cc, z, t] = wm[l, t]

        def mlp_b_start(l):
            for k in range(1, 4):
                remote(
                    wm.at[l, 0], GM.at[l, cc, z, peer_t(k)], ma[l] + k - 1, sib
                ).wait_recv()
            mlp_z[l][0]()

        def mlp_pass(l):
            mlp_z[l][1]()

        def mlp_c_copy(l, k):
            at = GM.at[l, cc, z_from(k)]
            return remote(at, at, mc[l] + k, sib)

        def mlp_c_start(l):
            mlp_c_copy(l, 0).start()
            mlp_c_copy(l, 2).start()
            for k in (1, 3):
                mlp_z[l][2](k)
                mlp_c_copy(l, k).start()

        def mlp_ready(l):
            for k in range(4):
                at = GM.at[l, 1 - cc, z_from(k)]
                remote(at, at, mc[l] + k, sib).wait_recv()
            for k in range(4):
                mlp_c_copy(l, k).wait_send()
            for k in range(1, 4):
                mlp_a_copy(l, k).wait_send()
            mlp_z[l][3]()

            def unpack(j, carry):
                jc = lax.rem(lax.div(j, 2), 2)
                jq = 2 * lax.div(j, 4) + lax.rem(j, 2)
                at = block(j)
                mixed = []
                for b in range(4):
                    chunk = GM[l, jc, b, jq]
                    W1[l, at, b * 128 : b * 128 + 128] = chunk[:, 0:128]
                    W2[l, at, b * 128 : b * 128 + 128] = chunk[:, 256:384]
                    mixed.append(chunk[:, 128:256].astype(F32))
                for b in range(2):
                    even, odd = mixed[2 * b], mixed[2 * b + 1]
                    lanes = slice(512 + b * 128, 640 + b * 128)
                    W1[l, at, lanes] = jnp.where(
                        lower, even, pltpu.roll(odd, 64, 1)
                    ).astype(BF16)
                    W2[l, at, lanes] = jnp.where(
                        lower, pltpu.roll(even, 64, 1), odd
                    ).astype(BF16)
                return carry

            lax.fori_loop(0, 8, unpack, 0)

        def rs_copy(i, k):
            return remote(RSS.at[k], RSR.at[i % 2, k - 1], rs_base[i] + k - 1, peer_dev(k))

        def rs_loop(i, order, part):
            def step(s, carry):
                k = order(s)
                partial = part(k)
                RSS[k] = partial.astype(BF16)

                @pl.when(k == 0)
                def _():
                    OWN[...] = partial

                @pl.when(k > 0)
                def _():
                    rs_copy(i, k).start()

                return carry

            lax.fori_loop(0, 4, step, 0)

        def rs_finish(i):
            for k in range(1, 4):
                rs_copy(i, k).wait_recv()
            total = OWN[...]
            for k in range(1, 4):
                total = total + RSR[i % 2, k - 1].astype(F32)
            for k in range(1, 4):
                rs_copy(i, k).wait_send()
            return total

        def ag_copy(i, buf, l, k):
            at = buf.at[l, rows(t)]
            return remote(at, at, ag_base[i] + k - 1, peer_dev(k))

        def ag_half(buf, l, k, upper):
            start = peer_t(k) * shard + upper * (shard // 2)
            return buf.at[l, pl.ds(pl.multiple_of(start, shard // 2), shard // 2)]

        def ag_relay(i, buf, l, k):
            at = ag_half(buf, l, k, k - 1)
            return remote(at, at, ag_base[i] + k + 1, peer_dev(3 - k))

        def ag_start(i, buf, l, value):
            buf[l, rows(t)] = value
            for k in (1, 2):
                ag_copy(i, buf, l, k).start()

        def ag_wait(i, buf, l, k):
            @pl.when(k == 1)
            def _():
                for near in (1, 2):
                    at = buf.at[l, rows(peer_t(near))]
                    remote(at, at, ag_base[i] + near - 1, sib).wait_recv()
                    ag_relay(i, buf, l, near).start()

            @pl.when(k == 3)
            def _():
                for upper in (0, 1):
                    at = ag_half(buf, l, 3, upper)
                    remote(at, at, ag_base[i] + 2 + upper, sib).wait_recv()

        def ag_drain(i, buf, l):
            for k in (1, 2):
                ag_copy(i, buf, l, k).wait_send()
                ag_relay(i, buf, l, k).wait_send()

        def forth(s):
            return s

        def back(s):
            return 3 - s

        def row(l, r):
            return shared[r, l : l + 1, :]

        def out_start(i, value):
            EZ[i, z] = value.astype(BF16)
            out_z[i][0]()

        def out_p_each(i, ks, act_far, act_near):
            for k in ks:
                zs = z_from(k)
                near = jnp.logical_and(lo == zs, y == cc)

                @pl.when(near)
                def _(zs=zs):
                    act_near(
                        pltpu.make_async_copy(
                            EZ.at[i, zs], (enc, xg)[i].at[t], lsem.at[2 + i]
                        )
                    )

                @pl.when(jnp.logical_not(near))
                def _(zs=zs, k=k):
                    act_far(
                        remote(
                            EZ.at[i, zs],
                            (enc, xg)[i].at[t],
                            op[i] + t,
                            {"dp": 4 * hi + zs, "seq": cc},
                            send=op[i] + k,
                        )
                    )

        def out_forward(i, ks):
            for k in ks:
                if k % 2 == 1:
                    out_z[i][2](k)
                out_p_each(i, (k,), lambda c: c.start(), lambda c: c.start())

        def out_finish(i, out):
            for d in range(4):
                mine = jnp.logical_and(t == d, cc == y)

                @pl.when(jnp.logical_not(mine))
                def _(d=d):
                    remote(EZ.at[i, 0], out.at[d], op[i] + d, sib).wait_recv()

            out_p_each(i, range(4), lambda c: c.wait_send(), lambda c: c.wait())
            out_z[i][3]()

        def att_grad_c_copy(l):
            return remote(SA.at[1 - cc], CA, gac[l], sib)

        def att_grad_a_copy(l, k):
            return remote(
                SA.at[cc, peer_t(k)], RA.at[l, t], gaa[l] + k - 1, peer_dev(k)
            )

        att_sum = [
            sum_z(lambda b, l=l: RA.at[l, b], FA.at[l], lambda k, l=l: RB.at[l, k - 1], gab[l])
            for l in range(layers)
        ]
        mlp_sum = [
            sum_z(lambda b, l=l: GM.at[l, cc, b], FM.at[l], lambda k, l=l: BM.at[l, k - 1], gmb[l])
            for l in range(layers)
        ]

        def att_grad_a(l):
            att_grad_c_copy(l).wait_recv()

            def add(q, carry):
                SA[cc, q] = (
                    SA[cc, q].astype(F32) + CA[q].astype(F32)
                ).astype(BF16)
                return carry

            lax.fori_loop(0, 4, add, 0)
            for k in range(1, 4):
                att_grad_a_copy(l, k).start()
            RA[l, t] = SA[cc, t]
            att_grad_c_copy(l).wait_send()

        def att_grad_b(l):
            for k in range(1, 4):
                remote(
                    SA.at[0, 0], RA.at[l, peer_t(k)], gaa[l] + k - 1, sib
                ).wait_recv()
            att_sum[l][4]()
            att_sum[l][0]()
            for k in range(1, 4):
                att_grad_a_copy(l, k).wait_send()

        def att_grad_end(l):
            total = RA[l, z].astype(F32)
            att_sum[l][2]()
            for k in range(1, 4):
                total = total + RB[l, k - 1].astype(F32)
            gh_out[l, 0, :, :] = total[:, 0:192].astype(BF16)
            gh_out[l, 1, :, 0:128] = total[:, 256:384].astype(BF16)
            k2 = pltpu.roll(total[:, 128:256], 64, 1)[:, 0:64]
            gh_out[l, 1, :, 128:192] = k2.astype(BF16)
            gh_out[l, 2, :, :] = total[:, 384:576].astype(BF16)
            att_sum[l][3]()

        def out_grad_c_copy(l):
            return remote(SO.at[1 - cc], CO, goc[l], sib)

        def out_grad_a_copy(l, k):
            return remote(SO.at[cc, peer_t(k)], RO.at[l, k - 1], goa[l] + k - 1, peer_dev(k))

        def out_grad_b_copy(l, k):
            return remote(
                TO.at[z_to(k)], RP.at[l, k - 1], gob[l] + k - 1, {"tensor": z_to(k)}
            )

        def out_grads(l):
            def product(b, carry):
                lanes = pl.ds(pl.multiple_of(b * 128, 128), 128)
                W2[l, lanes, :] = dot_tn(GO[l, :, lanes], CF[l]).astype(BF16)
                return carry

            lax.fori_loop(0, 6, product, 0)

            def pack(j, carry):
                jc = lax.rem(lax.div(j, 2), 2)
                jq = 2 * lax.div(j, 4) + lax.rem(j, 2)
                SO[jc, jq] = W2[l, block(j), :]
                return carry

            lax.fori_loop(0, 8, pack, 0)
            out_grad_c_copy(l).start()

        def out_grad_a(l):
            out_grad_c_copy(l).wait_recv()

            def add(q, carry):
                SO[cc, q] = (SO[cc, q].astype(F32) + CO[q].astype(F32)).astype(BF16)
                return carry

            lax.fori_loop(0, 4, add, 0)
            for k in range(1, 4):
                out_grad_a_copy(l, k).start()
            out_grad_c_copy(l).wait_send()

        def out_grad_b(l):
            total = SO[cc, t].astype(F32)
            for k in range(1, 4):
                out_grad_a_copy(l, k).wait_recv()
                total = total + RO[l, k - 1].astype(F32)
            total = total.astype(BF16)
            for b in range(4):
                TO[b, :, 0:128] = total[:, b * 128 : b * 128 + 128]
                pair = 512 + (b // 2) * 128
                TO[b, :, 128:256] = total[:, pair : pair + 128]
            for k in range(1, 4):
                out_grad_b_copy(l, k).start()
            for k in range(1, 4):
                out_grad_a_copy(l, k).wait_send()

        def out_grad_end(l):
            total = TO[z].astype(F32)
            for k in range(1, 4):
                out_grad_b_copy(l, k).wait_recv()
                total = total + RP[l, k - 1].astype(F32)
            go_out[l, :, 0:128] = total[:, 0:128].astype(BF16)
            pair = total[:, 128:256]
            pair = jnp.where(lax.rem(z, 2) == 1, pltpu.roll(pair, 64, 1), pair)
            go_out[l, :, 128:192] = pair[:, 0:64].astype(BF16)
            for k in range(1, 4):
                out_grad_b_copy(l, k).wait_send()

        def mlp_grad_c_copy(l):
            return remote(GM.at[l, 1 - cc], CM, gmc[l], sib)

        def mlp_grad_a_copy(l, k):
            return remote(TM.at[peer_t(k)], UM.at[l, t], gma[l] + k - 1, peer_dev(k))

        def mlp_grad_b(l):
            mlp_grad_c_copy(l).wait_recv()

            def add(s, carry):
                zs, q = lax.div(s, 4), lax.rem(s, 4)
                GM[l, cc, zs, q] = (
                    GM[l, cc, zs, q].astype(F32) + CM[zs, q].astype(F32)
                ).astype(BF16)
                return carry

            lax.fori_loop(0, 16, add, 0)
            mlp_sum[l][4]()
            mlp_grad_c_copy(l).wait_send()

        def mlp_grad_a(l):
            mlp_sum[l][2]()
            for q in range(4):
                total = GM[l, cc, z, q].astype(F32)
                for k in range(1, 4):
                    total = total + BM[l, k - 1, q].astype(F32)
                TM[q] = total.astype(BF16)
            for k in range(1, 4):
                mlp_grad_a_copy(l, k).start()
            UM[l, t] = TM[t]

        def mlp_grad_end(l):
            for k in range(1, 4):
                remote(TM.at[0], UM.at[l, peer_t(k)], gma[l] + k - 1, sib).wait_recv()
            gm_out[l] = UM[l]
            for k in range(1, 4):
                mlp_grad_a_copy(l, k).wait_send()
            mlp_sum[l][3]()

        def mlp_grads(l):
            def product(b, carry):
                lanes = pl.ds(pl.multiple_of(b * 128, 128), 128)
                W2[l, lanes, :] = dot_tn(GY[l, :, lanes], H[l]).astype(BF16)
                W1[l, lanes, :] = dot_tn(N[l, :, lanes], GF[...]).astype(BF16)
                return carry

            lax.fori_loop(0, 6, product, 0)

            def pack(j, carry):
                jc = lax.rem(lax.div(j, 2), 2)
                jq = 2 * lax.div(j, 4) + lax.rem(j, 2)
                at = block(j)
                for b in range(4):
                    lanes = slice(b * 128, b * 128 + 128)
                    GM[l, jc, b, jq, :, 0:128] = W1[l, at, lanes]
                    GM[l, jc, b, jq, :, 256:384] = W2[l, at, lanes]
                for b in range(2):
                    lanes = slice(512 + b * 128, 640 + b * 128)
                    one, two = W1[l, at, lanes].astype(F32), W2[l, at, lanes].astype(F32)
                    GM[l, jc, 2 * b, jq, :, 128:256] = jnp.where(
                        lower, one, pltpu.roll(two, 64, 1)
                    ).astype(BF16)
                    GM[l, jc, 2 * b + 1, jq, :, 128:256] = jnp.where(
                        lower, pltpu.roll(one, 64, 1), two
                    ).astype(BF16)
                return carry

            lax.fori_loop(0, 8, pack, 0)
            mlp_grad_c_copy(l).start()
            SMALL[8 * l + 7 : 8 * l + 8, :] = jnp.sum(GF[...].astype(F32), axis=0, keepdims=True)

        def att_grads(l):
            def product(b, carry):
                lanes = pl.ds(pl.multiple_of(b * 128, 128), 128)
                W1[l, lanes, 0:640] = dot_tn(A[l, :, lanes], G[...]).astype(BF16)
                return carry

            lax.fori_loop(0, 6, product, 0)

            def pack(j, carry):
                jc = lax.rem(lax.div(j, 2), 2)
                jq = 2 * lax.div(j, 4) + lax.rem(j, 2)
                SA[jc, jq] = W1[l, block(j), 0:640]
                return carry

            lax.fori_loop(0, 8, pack, 0)
            att_grad_c_copy(l).start()
            SMALL[8 * l + 6 : 8 * l + 7, 0:640] = jnp.sum(G[...].astype(F32), axis=0, keepdims=True)
            SMALL[8 * l + 6 : 8 * l + 7, 640:768] = jnp.zeros((1, 128), F32)

        def sv_copy(k):
            return remote(SV.at[z], SV.at[z], sv_base + k - 1, {"tensor": z_to(k)})

        def biases_start():
            SV[z] = jnp.zeros((layers, 8, 256), F32)
            for l in range(layers):
                for r in range(6):
                    SV[z, l, r : r + 1, 0:192] = sv[r, l : l + 1, :]
            for k in range(1, 4):
                sv_copy(k).start()

        def biases_ready():
            for k in range(1, 4):
                remote(SV.at[z], SV.at[z_from(k)], sv_base + k - 1, sib).wait_recv()
            for l in range(layers):
                BQ[l, :, 0:256] = SV[t, l, 0:1, :]
                BQ[l, :, 256:384] = jnp.zeros((1, 128), F32)
                BQ[l, :, 384:640] = SV[t, l, 1:2, :]
                hidden = [SV[b, l, pl.ds(2 + t, 1), :] for b in range(4)]
                for b in range(4):
                    B1[l, :, b * 128 : b * 128 + 128] = hidden[b][:, 0:128]
                for b in range(2):
                    even, odd = hidden[2 * b][:, 128:256], hidden[2 * b + 1][:, 128:256]
                    B1[l, :, 512 + b * 128 : 640 + b * 128] = jnp.where(
                        lower, even, pltpu.roll(odd, 64, 1)
                    )
            for k in range(1, 4):
                sv_copy(k).wait_send()

        def sz_copy(k):
            return remote(SMALL, SZ.at[k - 1], sz_base + k - 1, {"tensor": z_to(k)})

        def sc_copy():
            return remote(SZ.at[0], SC, sc_base, sib)

        def sq_copy(k):
            return remote(SP.at[t], SP.at[t], sq_base + k - 1, peer_dev(k))

        def small_z():
            for k in range(1, 4):
                sz_copy(k).start()

        def small_c():
            for k in range(1, 4):
                sz_copy(k).wait_recv()
            SZ[0] = SMALL[...] + SZ[0] + SZ[1] + SZ[2]
            sc_copy().start()

        def small_q():
            sc_copy().wait_recv()
            SP[t] = SZ[0] + SC[...]
            for k in range(1, 4):
                sq_copy(k).start()

        def small_end():
            for k in range(1, 4):
                remote(SC, SP.at[peer_t(k)], sq_base + k - 1, sib).wait_recv()
            z_half = lax.div(z, 2)
            upper = lax.rem(z, 2)
            for l in range(layers):
                at = slice(8 * l, 8 * l + 6)
                total = SP[0, at] + SP[1, at] + SP[2, at] + SP[3, at]
                for r in range(6):
                    shared_out[r, l : l + 1, :] = total[r : r + 1]
                line = slice(8 * l + 6, 8 * l + 7)
                split_out[0, l : l + 1, :] = SP[z, line, 0:192]
                split_out[1, l : l + 1, :] = SP[z, line, 384:576]
                line = slice(8 * l + 7, 8 * l + 8)
                for r in range(4):
                    first = SP[r, line, pl.ds(pl.multiple_of(z * 128, 128), 128)]
                    pair = SP[
                        r, line, pl.ds(pl.multiple_of(512 + z_half * 128, 128), 128)
                    ]
                    pair = jnp.where(upper == 1, pltpu.roll(pair, 64, 1), pair)
                    split_out[2 + r, l : l + 1, 0:128] = first
                    split_out[2 + r, l : l + 1, 128:192] = pair[:, 0:64]
            for k in range(1, 4):
                sz_copy(k).wait_send()
                sq_copy(k).wait_send()
            sc_copy().wait_send()

        def qkv(i, l, gathered):
            def step(k, carry):
                if gathered:
                    ag_wait(i, A, l, k)
                tp = peer_t(k)
                at = rows(tp)
                here = pl.ds(pl.multiple_of(cc * tokens + tp * shard, shard), shard)
                made = dot(A[l, at], WA[l]) + BQ[l]
                q01 = made[:, 0:128].astype(BF16) * jnp.asarray(0.125, BF16)
                qk2 = made[:, 128:256]
                q2 = qk2.astype(BF16) * jnp.asarray(0.125, BF16)
                none = jnp.zeros_like(q01)
                QC[l, tp, 0:128] = jnp.where(lower, q01, none)
                QC[l, tp, 128:256] = jnp.where(lower, none, q01)
                QC[l, tp, 256:384] = jnp.where(lower, q2, none)
                v01 = made[:, 384:512]
                v2 = jnp.where(lower, 0.0, pltpu.roll(made[:, 512:640], 64, 1))
                KV[l, 0, here] = made[:, 256:384].astype(BF16)
                KV[l, 1, here] = pltpu.roll(qk2, 64, 1).astype(BF16)
                KV[l, 2, here] = v01.astype(BF16)
                KV[l, 3, here] = v2.astype(BF16)
                VT[l, cc, 0, :, at] = jnp.transpose(v01).astype(BF16)
                VT[l, cc, 1, :, at] = jnp.transpose(v2).astype(BF16)
                return carry

            lax.fori_loop(0, 4, step, 0)
            kv_copy(l).start()
            vt_copy(l, cc).start()

        def kv_copy(l):
            at = KV.at[l, :, pl.ds(pl.multiple_of(cc * tokens, tokens), tokens)]
            return remote(at, at, kv_base[l], sib)

        def vt_copy(l, c):
            return remote(VT.at[l, c], VT.at[l, c], kv_base[l] + 1, sib)

        def kv_wait(l):
            at = KV.at[l, :, pl.ds(pl.multiple_of((1 - cc) * tokens, tokens), tokens)]
            remote(at, at, kv_base[l], sib).wait_recv()
            vt_copy(l, 1 - cc).wait_recv()

        def kv_drain(l):
            kv_copy(l).wait_send()
            vt_copy(l, cc).wait_send()

        def attend(l, hook=None):
            def weigh(scores):
                highest = jnp.max(scores, axis=0, keepdims=True)
                raised = jnp.exp(scores - highest)
                return raised.astype(BF16), 1.0 / jnp.sum(raised, axis=0, keepdims=True)

            def mix(tile, low):
                return dot(VT[l, 0, tile], low[0:tokens]) + dot(VT[l, 1, tile], low[tokens:])

            def step(s, carry):
                k = back(s)
                tp = peer_t(k)
                low, scale = weigh(dot_nt(KV[l, 0], QC[l, tp, 0:256]))
                E01[l, tp] = low
                RR[l, tp, :, 0:256] = scale
                made = mix(0, low) * scale
                both = jnp.where(top_rows, made[:, 0:128], made[:, 128:256])
                CS[k, 0:shard] = jnp.transpose(both).astype(BF16)
                low, scale = weigh(dot_nt(KV[l, 1], QC[l, tp, 256:384]))
                E2[l, tp] = low
                RR[l, tp, :, 256:384] = scale
                third = jnp.transpose(mix(1, low) * scale)
                half = shard // 2
                third = jnp.where(lower, pltpu.roll(third[0:half], 64, 1), third[half:shard])
                CS[k, shard : shard + half] = third.astype(BF16)

                @pl.when(k > 0)
                def _():
                    context_copy(l, k).start()

                if hook is not None:
                    pl.when(k == 1)(hook)
                return carry

            lax.fori_loop(0, 4, step, 0)
            CX[l, t] = CS[0]

        def context_copy(l, k):
            return remote(CS.at[k], CX.at[l, t], cx_base[l] + k - 1, peer_dev(k))

        def attended(l):
            for k in range(1, 4):
                remote(CS.at[0], CX.at[l, peer_t(k)], cx_base[l] + k - 1, sib).wait_recv()
            for b in range(4):
                CF[l, :, b * 128 : b * 128 + 128] = CX[l, b, 0:shard]
            half = shard // 2
            for b in range(2):
                even = CX[l, 2 * b, shard : shard + half].astype(F32)
                odd = CX[l, 2 * b + 1, shard : shard + half].astype(F32)
                lanes = slice(512 + b * 128, 640 + b * 128)
                first = jnp.where(lower, even, pltpu.roll(odd, 64, 1))
                second = jnp.where(lower, pltpu.roll(even, 64, 1), odd)
                CF[l, 0:half, lanes] = first.astype(BF16)
                CF[l, half:shard, lanes] = second.astype(BF16)
            for k in range(1, 4):
                context_copy(l, k).wait_send()
            return dot_nt(CF[l], WO[l])

        def turn(weight, l):
            def step(b, carry):
                at = pl.ds(pl.multiple_of(b * 128, 128), 128)
                wide = jnp.transpose(weight[l, at, :].astype(F32)).astype(BF16)
                T[0 : wide.shape[0], at] = wide
                return carry

            lax.fori_loop(0, width // 128, step, 0)

        def expand(i_ag, i_rs, l):
            def part(k):
                ag_wait(i_ag, N, l, k)
                at = rows(peer_t(k))
                f = dot(N[l, at], W1[l]) + B1[l]
                cdf = 0.5 * (1.0 + lax.erf(f * (2.0**-0.5)))
                slope = cdf + f * jnp.exp(-0.5 * f * f) * ((2.0 * math.pi) ** -0.5)
                H[l, at] = (f * cdf).astype(BF16)
                DG[l, at] = slope.astype(BF16)
                return dot(H[l, at], T[...])

            rs_loop(i_rs, forth, part)

        def shrink_back(i_ag, i_rs, l, gathered):
            def part(k):
                if gathered:
                    ag_wait(i_ag, GY, l, k)
                at = rows(peer_t(k))
                g = dot(GY[l, at], W2[l]) * DG[l, at].astype(F32)
                GF[at, :] = g.astype(BF16)
                return dot(GF[at, :], T[...])

            rs_loop(i_rs, forth, part)

        def context_grad_copy(l, k):
            return remote(CS.at[k], GC.at[l, t], gc_base[l] + k - 1, peer_dev(k))

        def context_grads(l, value):
            GO[l] = value
            made = dot(value, WO[l])
            half = shard // 2
            for b in range(4):
                CX[l, b, 0:shard] = made[:, b * 128 : b * 128 + 128].astype(BF16)
                pair = made[:, 512 + (b // 2) * 128 : 640 + (b // 2) * 128]
                first, second = pair[0:half], pair[half:shard]
                if b % 2 == 0:
                    both = jnp.where(lower, first, pltpu.roll(second, 64, 1))
                else:
                    both = jnp.where(lower, pltpu.roll(first, 64, 1), second)
                CX[l, b, shard : shard + half] = both.astype(BF16)
            for k in (3, 1, 2):
                CS[k] = CX[l, peer_t(k)]
                context_grad_copy(l, k).start()
            GC[l, t] = CX[l, t]

        def attend_back(l, hook):
            GKV[...] = jnp.zeros_like(GKV)
            for tile in range(2):
                for half in range(2):
                    keys = KV[l, tile, half * tokens : (half + 1) * tokens]
                    VT[0, half, tile] = jnp.transpose(keys.astype(F32)).astype(BF16)

            def step(k, carry):
                tp = peer_t(k)
                at = rows(tp)

                @pl.when(k > 0)
                def _():
                    remote(
                        CS.at[0], GC.at[l, tp], gc_base[l] + k - 1, sib
                    ).wait_recv()

                pl.when(k == 1)(hook)
                scale = RR[l, tp]
                r01, r2 = scale[:, 0:256], scale[:, 256:384]
                spread = jnp.where(top_rows, scale[:, 0:128], scale[:, 128:256])
                by_row = jnp.transpose(spread)
                by_row2 = jnp.transpose(jnp.where(top_rows, 0.0, r2))
                c01 = (GC[l, tp, 0:shard].astype(F32) * by_row).astype(BF16)
                third = GC[l, tp, shard : shard + shard // 2].astype(F32)
                third = jnp.concatenate([pltpu.roll(third, 64, 1), third], axis=0)
                c2 = (third * by_row2).astype(BF16)
                none = jnp.zeros_like(c01)
                c01 = jnp.concatenate(
                    [jnp.where(lower, c01, none), jnp.where(lower, none, c01)], axis=0
                )
                made = []
                for tile, low_ref, scale, grad, lanes in (
                    (0, E01, r01, c01, slice(0, 256)),
                    (1, E2, r2, c2, slice(256, 384)),
                ):
                    gp = dot_nt(KV[l, 2 + tile], grad)
                    low = low_ref[l, tp]
                    e = low.astype(F32)
                    inner = scale * jnp.sum(e * gp, axis=0, keepdims=True)
                    gs = (e * (gp - inner)).astype(BF16)
                    GKV[tile] += dot(gs, QC[l, tp, lanes])
                    GKV[2 + tile] += dot(low, grad)
                    made.append(dot(VT[0, 0, tile], gs[0:tokens]) + dot(VT[0, 1, tile], gs[tokens:]))
                both = jnp.where(top_rows, made[0][:, 0:128], made[0][:, 128:256])
                GQ[at, 0:128] = (0.125 * jnp.transpose(both)).astype(BF16)
                third = jnp.where(lower, 0.125 * jnp.transpose(made[1]), 0.0)
                GQ[at, 128:256] = third.astype(BF16)
                return carry

            lax.fori_loop(0, 4, step, 0)
            other = pl.ds(pl.multiple_of((1 - cc) * tokens, tokens), tokens)
            for tile in range(4):
                KVS[tile] = GKV[tile, other].astype(BF16)
            gkv_copy(l).start()
            for k in range(1, 4):
                context_grad_copy(l, k).wait_send()

        def gkv_copy(l):
            return remote(KVS, KVR.at[l], gkv_base[l], sib)

        def heads_back(i, l):
            gkv_copy(l).wait_recv()
            gkv_copy(l).wait_send()

            def part(k):
                at = rows(peer_t(k))
                here = pl.ds(pl.multiple_of(cc * tokens + peer_t(k) * shard, shard), shard)
                k01, k2, v01, v2 = (
                    GKV[tile, here] + KVR[l, tile, at].astype(F32) for tile in range(4)
                )
                G[at, 0:128] = GQ[at, 0:128]
                G[at, 128:256] = (
                    GQ[at, 128:256].astype(F32) + pltpu.roll(k2, 64, 1)
                ).astype(BF16)
                G[at, 256:384] = k01.astype(BF16)
                G[at, 384:512] = v01.astype(BF16)
                G[at, 512:640] = pltpu.roll(v2, 64, 1).astype(BF16)
                return dot(G[at, :], T[0:640, :])

            rs_loop(i, back, part)

        spread_start(frames, X0, 0)
        att_b_start(0)
        att_a_piece(0, 0)
        biases_start()
        mlp_a_start(0)
        for p in range(4):
            spread_pass(X0, 0, p)
        for p in range(4):
            spread_wait(frames, X0, 0, p)
        att_a_first(0)

        def first_norm(k, carry):
            at = rows(k)
            hat, inverse = norm_parts(X0[at, :].astype(F32))
            A[0, at] = (hat * row(0, 0) + row(0, 1)).astype(BF16)
            return carry

        lax.fori_loop(0, 4, first_norm, 0)
        XS[0] = X0[rows(t), :].astype(F32)
        att_a_rest(0)
        out_b_start(0)
        mlp_b_start(0)
        biases_ready()
        att_c_start(0)
        att_ready(0)
        spread_start(cot, GY.at[top], 1)
        for l in range(layers):
            qkv(4 * l + 3, l, l > 0)
            out_a_start(l)
            kv_wait(l)
            if l == 0:
                for p in range(4):
                    spread_pass(GY.at[top], 1, p)
            attend(l, (lambda: mlp_pass(0)) if l == 0 else None)
            out_c_start(l)
            if l > 0:
                mlp_pass(l)
            out_ready(l)
            between = XS[l] + attended(l) + row(l, 2)
            MS[l] = between
            hat, inverse = norm_parts(between)
            ag_start(4 * l, N, l, (hat * row(l, 3) + row(l, 4)).astype(BF16))
            mlp_c_start(l)
            mlp_ready(l)
            if l + 1 < layers:
                att_b_start(l + 1)
                out_b_start(l + 1)
            turn(W2, l)
            expand(4 * l, l, l)
            if l + 1 < layers:
                mlp_a_start(l + 1)
                att_a_piece(l + 1, 0)
                att_a_first(l + 1)
                att_a_rest(l + 1)
                mlp_b_start(l + 1)
                total = rs_finish(l)
                stream = MS[l] + total + row(l, 5)
                XS[l + 1] = stream
                hat, inverse = norm_parts(stream)
                normed = (hat * row(l + 1, 0) + row(l + 1, 1)).astype(BF16)
                ag_start(4 * l + 7, A, l + 1, normed)
                att_c_start(l + 1)
                att_ready(l + 1)
            else:
                turn(W1, l)
                total = rs_finish(l)
                out_start(0, MS[l] + total + row(l, 5))

        spread_drain(frames, X0, 0)
        for l in range(layers):
            kv_drain(l)
        for p in range(4):
            spread_wait(cot, GY.at[top], 1, p)
        GS[...] = GY[top, rows(t)].astype(F32)
        rs_next = layers
        for l in reversed(range(layers)):
            shrink_back(4 * l + 2, rs_next, l, l < top)
            mlp_grads(l)
            mlp_grad_b(l)
            mlp_sum[l][0]()
            grad = GS[...]
            SMALL[8 * l + 5 : 8 * l + 6, :] = jnp.sum(grad, axis=0, keepdims=True)
            gn = rs_finish(rs_next)
            rs_next += 1
            hat, inverse = norm_parts(MS[l])
            gm = grad + norm_back(gn, hat, inverse, row(l, 3))
            context_grads(l, gm.astype(BF16))
            GS[...] = gm
            SMALL[8 * l + 3 : 8 * l + 4, :] = jnp.sum(gn * hat, axis=0, keepdims=True)
            SMALL[8 * l + 4 : 8 * l + 5, :] = jnp.sum(gn, axis=0, keepdims=True)
            SMALL[8 * l + 2 : 8 * l + 3, :] = jnp.sum(gm, axis=0, keepdims=True)
            if l < top:
                att_grad_a(l + 1)
            out_grads(l)

            def hook(l=l):
                if l == top:
                    out_z[0][1]()
                    out_forward(0, (0, 2))
                out_grad_a(l)

            attend_back(l, hook)
            if l < top:
                att_grad_b(l + 1)
            turn(WA, l)
            heads_back(rs_next, l)
            mlp_sum[l][1]()
            att_grads(l)
            out_grad_b(l)
            if l < top:
                att_sum[l + 1][1]()
            if l == 0:
                att_grad_a(l)
            gn = rs_finish(rs_next)
            rs_next += 1
            hat, inverse = norm_parts(XS[l])
            gx = GS[...] + norm_back(gn, hat, inverse, row(l, 0))
            if l > 0:
                ag_start(4 * l - 2, GY, l - 1, gx.astype(BF16))
                GS[...] = gx
            SMALL[8 * l : 8 * l + 1, :] = jnp.sum(gn * hat, axis=0, keepdims=True)
            SMALL[8 * l + 1 : 8 * l + 2, :] = jnp.sum(gn, axis=0, keepdims=True)
            if l == 0:
                small_z()
                out_start(1, gx)
                out_forward(1, (0,))
            else:
                turn(W1, l - 1)
                out_grad_end(l)
        small_c()
        att_grad_b(0)
        if layers > 1:
            mlp_grad_a(1)
        out_forward(0, (1, 3))
        small_q()
        out_z[1][1]()
        out_forward(1, (2,))
        att_sum[0][1]()
        if layers > 1:
            mlp_grad_end(1)
        mlp_grad_a(0)
        out_forward(1, (1, 3))
        if layers > 1:
            att_grad_end(1)
        mlp_grad_end(0)
        out_grad_end(0)
        small_end()
        out_finish(0, enc)
        att_grad_end(0)
        out_finish(1, xg)

        spread_drain(cot, GY.at[top], 1)
        for l in range(layers):
            att_drain(l)
            ag_drain(4 * l, N, l)
            out_drain(l)
            if l < top:
                ag_drain(4 * l + 2, GY, l)
            if l > 0:
                ag_drain(4 * l + 3, A, l)

    return kernel


def fused_step(frames, cot, hw, mw, wm, shared, sv):
    layers, rows_of, _ = mw.shape
    tokens, width = frames.shape
    shard = tokens // 4
    numbers = Numbers()
    kernel = make_kernel(layers, tokens, width, numbers)
    two = 2 * tokens
    v = pltpu.VMEM
    scratch = [
        v((layers, shard, width), F32),
        v((layers, shard, width), F32),
        v((layers, tokens, width), BF16),
        v((layers, tokens, width), BF16),
        v((layers, shard, width), BF16),
        v((layers, tokens, width), BF16),
        v((shard, width), F32),
        v((layers, width, 640), BF16),
        v((layers, width, width), BF16),
        v((layers, width, width), BF16),
        v((layers, width, width), BF16),
        v((width, width), BF16),
        v((layers, 4, rows_of, 640), BF16),
        v((layers, 4, rows_of, 256), BF16),
        v((layers, 2, 4, 4, rows_of, width // 2), BF16),
        v((layers, 4, 3 * shard, 128), BF16),
        v((layers, 4, two, 128), BF16),
        v((layers, 2, 2, 128, tokens), BF16),
        v((layers, 4, two, 2 * shard), BF16),
        v((layers, 4, two, shard), BF16),
        v((layers, 4, 1, 3 * shard), F32),
        v((4, 3 * shard // 2, 128), BF16),
        v((layers, 4, 3 * shard // 2, 128), BF16),
        v((layers, shard, width), BF16),
        v((layers, 4, 3 * shard // 2, 128), BF16),
        v((layers, tokens, width), BF16),
        v((layers, tokens, width), BF16),
        v((tokens, width), BF16),
        v((tokens, 256), BF16),
        v((tokens, 640), BF16),
        v((4, two, 128), F32),
        v((4, tokens, 128), BF16),
        v((layers, 4, tokens, 128), BF16),
        v((shard, width), F32),
        v((4, shard, width), BF16),
        v((2, 3, shard, width), BF16),
        v((4, 4, rows_of, width // 2), BF16),
        v((layers, 3, 4, rows_of, width // 2), BF16),
        v((4, rows_of, width // 2), BF16),
        v((layers, 4, rows_of, width // 2), BF16),
        v((layers, 4, rows_of, width // 2), BF16),
        v((layers, rows_of, 640), BF16),
        v((2, 4, rows_of, 640), BF16),
        v((4, rows_of, 640), BF16),
        v((layers, 4, rows_of, 640), BF16),
        v((layers, 3, rows_of, 640), BF16),
        v((2, 4, rows_of, width), BF16),
        v((4, rows_of, width), BF16),
        v((layers, 3, rows_of, width), BF16),
        v((4, rows_of, 256), BF16),
        v((layers, 3, rows_of, 256), BF16),
        v((2, 4, shard, width), BF16),
        v((4, layers, 8, 256), F32),
        v((layers, 1, 640), F32),
        v((layers, 1, width), F32),
        v((8 * layers, width), F32),
        v((3, 8 * layers, width), F32),
        v((8 * layers, width), F32),
        v((4, 8 * layers, width), F32),
        pltpu.SemaphoreType.DMA((numbers.count,)),
        pltpu.SemaphoreType.DMA((numbers.count,)),
        pltpu.SemaphoreType.DMA((4,)),
    ]
    inside = pl.BlockSpec(memory_space=pltpu.VMEM)
    outside = pl.BlockSpec(memory_space=pl.ANY)
    return pl.pallas_call(
        kernel,
        out_shape=(
            jax.ShapeDtypeStruct((4, shard, width), BF16),
            jax.ShapeDtypeStruct((4, shard, width), BF16),
            jax.ShapeDtypeStruct((layers, 3, rows_of, width // 4), BF16),
            jax.ShapeDtypeStruct((layers, rows_of, width // 4), BF16),
            jax.ShapeDtypeStruct((layers, 4, rows_of, width // 2), BF16),
            jax.ShapeDtypeStruct((6, layers, width), F32),
            jax.ShapeDtypeStruct((6, layers, width // 4), F32),
        ),
        in_specs=[outside, outside] + [inside] * 5,
        out_specs=(outside, outside) + (inside,) * 5,
        scratch_shapes=scratch,
        compiler_params=pltpu.CompilerParams(
            collective_id=0, has_side_effects=True, vmem_limit_bytes=63 * 1024 * 1024
        ),
    )(frames, cot, hw, mw, wm, shared, sv)


def adam_update(weight, gradient, first_moment, second, step_rate):
    first_new = beta_one * first_moment + (1.0 - beta_one) * gradient
    second_new = beta_two * second + (1.0 - beta_two) * gradient * gradient
    bias_one = 1.0 - beta_one**STEP
    bias_two = 1.0 - beta_two**STEP
    direction = first_new / bias_one / (jnp.sqrt(second_new / bias_two) + adam_epsilon)
    return (second_new, weight - step_rate * (direction + weight_decay * weight))


RATES = (0.1, 0.1, 0.1, 0.1, 2.0, 0.5)


def finish_kernel(*refs):
    enc, xg, pairs = refs[0:3]
    outs = refs[25:]
    groups, at = [], 3
    for i in range(6):
        packed = i in (2, 3)
        grad = (outs[2 + 3 * i],) if packed else (refs[at],)
        at += 0 if packed else 1
        groups.append(grad + tuple(refs[at : at + 3]))
        at += 3
    for r in range(4):
        total = pairs[0, r].astype(F32)
        third = pltpu.roll(total[:, 128:256], 64, 1)
        outs[8][0, :, r, :] = total[:, 0:192]
        outs[11][0, :, r, 0:128] = total[:, 256:384]
        outs[11][0, :, r, 128:192] = third[:, 0:64]
    outs[0][...] = enc[...].astype(F32)
    outs[1][...] = xg[...].astype(F32)
    for i, (grad, weight, first, second) in enumerate(groups):
        g = grad[...].astype(F32)
        renewed, updated = adam_update(weight[...], g, first[...], second[...], RATES[i])
        if i not in (2, 3):
            outs[2 + 3 * i][...] = g
        outs[3 + 3 * i][...] = renewed
        outs[4 + 3 * i][...] = updated


def finish(enc, xg, pairs, groups):
    layers, _, rows_of, wide = groups[0][0].shape
    tokens, width = enc.shape
    cut = 2 if rows_of % 16 == 0 else 1
    steps = layers * cut
    part = rows_of // cut
    stream = pl.BlockSpec((tokens // steps, width), lambda l, h: (cut * l + h, 0))
    heads = pl.BlockSpec((1, 3, part, wide), lambda l, h: (l, 0, h, 0))
    flat = pl.BlockSpec((1, part, wide), lambda l, h: (l, h, 0))
    grid = pl.BlockSpec((1, part, 4, wide), lambda l, h: (l, h, 0, 0))
    shared = pl.BlockSpec((6, layers, width), lambda l, h: (0, 0, 0))
    split = pl.BlockSpec((6, layers, wide), lambda l, h: (0, 0, 0))
    kinds = (heads, flat, grid, grid, shared, split)
    both = pl.BlockSpec((1, 4, part, 2 * wide), lambda l, h: (l, 0, h, 0))
    shapes = [jax.ShapeDtypeStruct((tokens, width), F32)] * 2
    out_specs = [stream, stream]
    for kind, group in zip(kinds, groups):
        shapes += [jax.ShapeDtypeStruct(group[-1].shape, F32)] * 3
        out_specs += [kind] * 3
    return pl.pallas_call(
        finish_kernel,
        grid=(layers, cut),
        out_shape=shapes,
        in_specs=[stream, stream, both]
        + [kind for kind, group in zip(kinds, groups) for _ in group],
        out_specs=out_specs,
        compiler_params=pltpu.CompilerParams(
            dimension_semantics=("arbitrary", "arbitrary"),
            vmem_limit_bytes=63 * 1024 * 1024,
        ),
    )(enc, xg, pairs, *[v for group in groups for v in group])


def shards(
    frames, cotangent, heads_weight, merge_weight, expand_weight, shrink_weight,
    shared_vectors, split_vectors,
    heads_first, heads_second, merge_first, merge_second, expand_first, expand_second,
    shrink_first, shrink_second, shared_first, shared_second, split_first, split_second,
):
    groups = lax.axis_size("dp") // 4
    width = frames.shape[-1]
    dp_group = [[lo + 4 * h for h in range(groups)] for lo in range(4)]

    def to_kernel(v):
        if groups == 1:
            return v
        part = v.reshape(v.shape[:-1] + (groups, 8, width // (8 * groups)))
        return jnp.swapaxes(part, -3, -2).reshape(v.shape)

    def from_kernel(v):
        if groups == 1:
            return v
        part = v.reshape(v.shape[:-1] + (8, groups, width // (8 * groups)))
        return jnp.swapaxes(part, -3, -2).reshape(v.shape)

    def widen(v, axis):
        if groups == 1:
            return v
        return lax.all_gather(
            v, "dp", axis=axis, tiled=True, axis_index_groups=dp_group
        )

    def narrow(v, axis):
        if groups == 1:
            return v
        return lax.psum_scatter(
            v.astype(BF16),
            "dp",
            scatter_dimension=axis,
            tiled=True,
            axis_index_groups=dp_group,
        ).astype(F32)

    e = jnp.swapaxes(expand_weight.astype(BF16), 1, 2)
    s = jnp.swapaxes(shrink_weight.astype(BF16), 1, 2)
    wm = jnp.concatenate([e, s[..., 128:], s[..., :128]], axis=-1)
    wm = widen(wm, 2)
    hw, mw = jnp.swapaxes(heads_weight, 1, 2), merge_weight
    if groups > 1:
        hw = widen(hw.astype(BF16), 2).astype(F32)
        mw = widen(mw.astype(BF16), 1).astype(F32)

    enc, xg, heads_grad, merge_grad, pairs, shared_grad, split_grad = (
        fused_step(
            to_kernel(frames[0]),
            to_kernel(cotangent[0]),
            hw,
            mw,
            wm,
            jnp.swapaxes(to_kernel(shared_vectors), 0, 1),
            jnp.swapaxes(split_vectors, 0, 1),
        )
    )
    enc, xg = (from_kernel(v.reshape(frames.shape[1:])) for v in (enc, xg))
    heads_grad = narrow(heads_grad, 2)
    merge_grad = narrow(merge_grad, 1)
    pairs = narrow(pairs, 2)
    shared_grad = from_kernel(shared_grad)
    if groups > 1:
        shared_grad = lax.psum(shared_grad, "dp", axis_index_groups=dp_group)
        split_grad = lax.psum(split_grad, "dp", axis_index_groups=dp_group)

    def turned(v):
        return jnp.swapaxes(v, 1, 2)

    def lined(v):
        return jnp.swapaxes(v, 0, 1)

    def same(v):
        return v

    table = (
        (turned, (heads_grad,), heads_weight, heads_first, heads_second),
        (same, (merge_grad,), merge_weight, merge_first, merge_second),
        (same, (), expand_weight, expand_first, expand_second),
        (same, (), shrink_weight, shrink_first, shrink_second),
        (lined, (shared_grad,), shared_vectors, shared_first, shared_second),
        (lined, (split_grad,), split_vectors, split_first, split_second),
    )
    groups_in = [g + tuple(view(v) for v in rest) for view, g, *rest in table]
    done = finish(enc, xg, pairs, groups_in)
    out = [done[0][None], done[1][None]]
    for i, (view, *_) in enumerate(table):
        out += [view(v) for v in done[2 + 3 * i : 5 + 3 * i]]
    return tuple(out)


def solution(mesh):
    rows = ("dp", "seq")
    stream = P("dp", "seq", None)
    wide = P(None, rows, None, "tensor")
    flat = P(None, rows, "tensor")
    split = P(None, None, "tensor")
    return jax.shard_map(
        shards,
        mesh=mesh,
        in_specs=(
            stream, stream, wide, flat, wide, wide, P(), split,
            wide, wide, flat, flat, wide, wide, wide, wide, P(), P(), split, split,
        ),
        out_specs=(stream, stream)
        + (wide,) * 3 + (flat,) * 3 + (wide,) * 6 + (P(),) * 3 + (split,) * 3,
        check_vma=False,
    )
```
